512 devices in a mesh: grp: 16 (over z), tile: 8 (over x_hi, y), arch: 4 (over x_lo, core).
Axes of the slice: x: 4 (x_hi: 2, x_lo: 2; x = x_hi * 2 + x_lo), y: 4, z: 16, core: 2. Of those that a mesh axis runs over, the one named last changes fastest.
Arguments:
- query_grads: bfloat16 [4, 1536, 4096], P('arch', 'tile', 'grp'), may hold values from -6 to 6
- input_basis: bfloat16 [4096, 4096], P(None, 'grp'), may hold values from -0.09375 to 0.09375
- output_basis: bfloat16 [1536, 1536], P(None, 'tile'), may hold values from -0.15625 to 0.15625
- eigenvalues: float32 [1536, 4096], P('tile', 'grp'), may hold values from 0.1 to 10
- activations: bfloat16 [1024, 4096], P('arch', 'grp'), may hold values from -6 to 6
- gradients: bfloat16 [1024, 1536], P('arch', 'tile'), may hold values from -0.0099487305 to 0.0099487305
- seq_lengths: int32 [4, 8], P('arch'), may hold values from 1 to 128, 256 in all within a row
Outputs:
- preconditioned: bfloat16 [4, 4096, 1536], P('arch', 'grp', 'tile')
- sequence_scores: float32 [4, 32], P(None, 'arch')
The draws below stay inside these ranges and needn't reach their ends.
Inputs may be any that keep to these rules, and one draw needn't show every extreme that they name: Each row of seq_lengths sums to 256, and its largest entry is exactly 128.
All inputs are finite; a program needn't handle non-finite values.
Results may differ from the reference program's by a relative error of at most 0.013.
Values may be sent and summed in bfloat16 or wider, within the bound.
A program may use at most 64 MiB of HBM per device.

```python
import math
import jax
import jax.numpy as jnp
import numpy as np
from jax import lax

D = 4096
F = 1536
NQ = 4
ROWS_DEV = 256
SEQS_DEV = 8
ROWS = 1024
MOST = 128
N_TILE = 8
N_ARCH = 4


def block_scale(key, extent, shards, least, high):
    level = 1.0
    for dim, shards_of in shards:
        steps = jax.random.uniform(jax.random.fold_in(jax.random.fold_in(key, 6), dim), (shards_of,), jnp.float32, least / len(shards), high / len(shards))
        level = level * jnp.repeat(jnp.exp(steps), extent[dim] // shards_of).reshape((-1,) + (1,) * (len(extent) - 1 - dim))
    return level


def profile(count, total, most, lean):
    portions = [(1 << 20) // math.isqrt(rank ** lean) + 1 for rank in range(2, count + 1)]
    spare, given = total - most - (count - 1), [1] * (count - 1)
    while spare > 0:
        free = [i for i in range(count - 1) if given[i] < most]
        whole, remaining = sum([portions[i] for i in free]), spare
        for i in free:
            more = min(most - given[i], max(1, remaining * portions[i] // whole), spare)
            given[i] = given[i] + more
            spare = spare - more
    return np.array([most] + given)


def uneven(own_key, amount, total, bound, skew):
    if amount == 2:
        one = jax.random.randint(own_key, (), max(1, total - bound), min(bound, total - 1) + 1)
        return jnp.stack([one, total - one])
    lengths = jnp.asarray(profile(amount, total, bound, skew), jnp.int32)
    couples = (amount - 1) // 2
    donor, taker = lengths[1:1 + 2 * couples:2], lengths[2:2 + 2 * couples:2]
    slack = jnp.minimum(donor - 1, bound - taker)
    passed = jax.random.randint(jax.random.fold_in(own_key, 1), (couples,), 0, 1 << 20) % (slack + 1)
    lengths = lengths.at[1:1 + 2 * couples:2].set(donor - passed).at[2:2 + 2 * couples:2].set(taker + passed)
    return lengths[jax.random.permutation(jax.random.fold_in(own_key, 2), amount)]


def bell_draw(rng, extent, deviation, limit, shards=(), held_as=jnp.bfloat16):
    values = deviation * jax.random.normal(rng, extent, jnp.float32)
    if shards:
        values = values * block_scale(rng, extent, shards, -0.22, 0.18)
    return jnp.clip(values, -limit, limit).astype(held_as)


def setup_inputs(seed: int = 0) -> dict:
    keys = jax.random.split(jax.random.key(seed), 8)
    return {
        "query_grads": bell_draw(keys[0], (NQ, F, D), 1.0, 6.0, ((0, 4), (1, 8), (2, 16))),
        "input_basis": bell_draw(keys[1], (D, D), D ** -0.5, 0.09375, ((1, 16),)),
        "output_basis": bell_draw(keys[2], (F, F), F ** -0.5, 0.15625, ((1, 8),)),
        "eigenvalues": jnp.clip(jnp.exp(math.log(10.0) - 4.6051702 * jax.random.uniform(keys[3], (F, D), jnp.float32) ** block_scale(keys[3], (F, D), ((0, 8), (1, 16)), -0.2, 0.2)), 0.1, 10.0),
        "activations": bell_draw(keys[4], (ROWS, D), 1.0, 6.0, ((0, 4), (1, 16))),
        "gradients": bell_draw(keys[5], (ROWS, F), 0.0015, 0.0099487305, ((0, 4), (1, 8))),
        "seq_lengths": jax.vmap(lambda own: uneven(own, SEQS_DEV, ROWS_DEV, MOST, 1))(jax.random.split(keys[6], N_ARCH)).reshape((N_ARCH, SEQS_DEV)).astype(jnp.int32),
    }


damping = 0.01


def reference(query_grads, input_basis, output_basis, eigenvalues, activations, gradients, seq_lengths):
    block = F // N_TILE
    grads_f = gradients.astype(jnp.float32)
    pre_list = []
    score_list = []
    for query in range(NQ):
        rotated_in = jnp.dot(query_grads[query], input_basis, preferred_element_type=jnp.float32).astype(jnp.bfloat16)
        rotated = jnp.dot(output_basis.T, rotated_in, preferred_element_type=jnp.float32)
        scaled = (rotated / (eigenvalues + damping)).astype(jnp.bfloat16)
        restored = jnp.zeros((F, D), jnp.float32)
        for index in range(N_TILE):
            product = jnp.dot(output_basis[:, index * block:(index + 1) * block], scaled[index * block:(index + 1) * block, :], preferred_element_type=jnp.float32)
            restored = restored + lax.optimization_barrier(product.astype(jnp.bfloat16)).astype(jnp.float32)
        restored = restored.astype(jnp.bfloat16)
        precond = jnp.dot(input_basis, restored.T, preferred_element_type=jnp.float32).astype(jnp.bfloat16)
        pre_list.append(precond)
        projected = jnp.dot(activations, precond, preferred_element_type=jnp.float32)
        score_list.append(jnp.sum(projected * grads_f, axis=1))
    preconditioned = jnp.stack(pre_list, axis=0)
    token_scores = jnp.stack(score_list, axis=0).reshape(NQ, N_ARCH, ROWS_DEV)
    ends = jnp.cumsum(seq_lengths, axis=1)
    starts = ends - seq_lengths
    position = jnp.arange(ROWS_DEV, dtype=jnp.int32)
    member = ((position[None, None, :] >= starts[:, :, None]) & (position[None, None, :] < ends[:, :, None])).astype(jnp.float32)
    totals = jnp.einsum("qar,asr->qas", token_scores, member, precision=lax.Precision.HIGHEST)
    sequence_scores = (totals / seq_lengths.astype(jnp.float32)[None, :, :]).reshape(NQ, N_ARCH * SEQS_DEV)
    return preconditioned, sequence_scores
```

```python
import functools

import jax
import jax.numpy as jnp
from jax import lax
from jax.experimental import pallas as pl
from jax.experimental.pallas import tpu as pltpu
from jax.sharding import PartitionSpec as P

damping = 0.01
MESH = pl.DeviceIdType.MESH


def dot(a, b):
    return jnp.dot(a, b, preferred_element_type=jnp.float32)


def dot_last(a, b):
    return lax.dot_general(a, b, (((1,), (1,)), ((), ())), preferred_element_type=jnp.float32)


def kernel(
    nz, nt, na,
    q_hbm, u_hbm, vt_hbm, eig_hbm, act_hbm, gt_hbm, len_ref,
    pre_ref, score_ref,
    piece, from_left, from_right, u, vt, v, inv, gt,
    acc, rin, aprime, outgoing, arrived, rall, chain_a, chain_b, first,
    partial, seq_tile, seq_z,
    local_sem,
    zr_send, zr_recv, zl_send, zl_recv,
    t_send, t_recv, a_send, a_recv, s_send, s_recv,
    q_send, q_recv,
    rr_send, rr_recv, rl_send, rl_recv,
    pt_send, pt_recv, pz_send, pz_recv,
):
    z, t, a = lax.axis_index("grp"), lax.axis_index("tile"), lax.axis_index("arch")
    fb, db = q_hbm.shape[1], q_hbm.shape[2]
    half = fb // 2
    ra = act_hbm.shape[0] // nt
    rows = ((0, half), (half, fb - half + ra))
    reach = nz // 2
    right_reach, left_reach = (reach, reach - 1), (reach - 1, reach)

    def zdev(d):
        return {"grp": lax.rem(z + (d + nz), nz)}

    def tdev(j):
        return {"tile": lax.rem(t + j, nt)}

    def adev(j):
        return {"arch": lax.rem(a + j, na)}

    loads = [
        pltpu.make_async_copy(q_hbm.at[0], piece.at[pl.ds(0, fb)], local_sem.at[0]),
        pltpu.make_async_copy(
            act_hbm.at[pl.ds(pl.multiple_of(t * ra, ra), ra)], piece.at[pl.ds(fb, ra)], local_sem.at[1]
        ),
        pltpu.make_async_copy(u_hbm, u, local_sem.at[2]),
        pltpu.make_async_copy(vt_hbm, vt, local_sem.at[3]),
        pltpu.make_async_copy(eig_hbm, inv, local_sem.at[4]),
        pltpu.make_async_copy(gt_hbm, gt, local_sem.at[5]),
    ]
    for load in loads:
        load.start()

    barrier = pltpu.get_barrier_semaphore()
    peers = [zdev(d) for d in range(1, nz)] + [tdev(j) for j in range(1, nt)] + [adev(j) for j in range(1, na)]
    for peer in peers:
        pl.semaphore_signal(barrier, inc=1, device_id=peer, device_id_type=MESH)
    loads[0].wait()
    loads[1].wait()
    pl.semaphore_wait(barrier, len(peers))

    def remote(src, dst, send, recv, dev):
        return pltpu.make_async_remote_copy(
            src_ref=src, dst_ref=dst, send_sem=send, recv_sem=recv, device_id=dev, device_id_type=MESH
        )

    def gather_right(step, c):
        sl = pl.ds(*rows[c])
        src = piece.at[sl] if step == 0 else from_left.at[step - 1, sl]
        return remote(src, from_left.at[step, sl], zr_send.at[step, c], zr_recv.at[step, c], zdev(1))

    def gather_left(step, c):
        sl = pl.ds(*rows[c])
        src = piece.at[sl] if step == 0 else from_right.at[step - 1, sl]
        return remote(src, from_right.at[step, sl], zl_send.at[step, c], zl_recv.at[step, c], zdev(-1))

    sent = []

    def go(copy):
        copy.start()
        sent.append(copy)

    for c in range(2):
        go(gather_right(0, c))
        go(gather_left(0, c))

    def urows(d):
        k = lax.rem(z + (d + nz), nz)
        return pl.ds(pl.multiple_of(k * db, db), db)

    for load in loads[2:]:
        load.wait()
    acc[...] = dot(piece[...], u[urows(0), :])
    inv[...] = 1.0 / (inv[...] + damping)
    v[...] = vt[...].T

    def start_tile_gather(c):
        mine = pl.ds(pl.multiple_of(t * fb + c * half, 16), half)
        rin[mine, :] = acc[pl.ds(c * half, half), :].astype(jnp.bfloat16)
        for j in range(1, nt):
            go(remote(rin.at[mine], rin.at[mine], t_send.at[j, c], t_recv.at[j, c], tdev(j)))

    for step in range(reach):
        for c in range(2):
            sl = pl.ds(*rows[c])
            if step < right_reach[c]:
                gather_right(step, c).wait_recv()
                if step + 1 < right_reach[c]:
                    go(gather_right(step + 1, c))
            if step < left_reach[c]:
                gather_left(step, c).wait_recv()
                if step + 1 < left_reach[c]:
                    go(gather_left(step + 1, c))
            if step < right_reach[c]:
                acc[sl, :] += dot(from_left[step, sl, :], u[urows(-1 - step), :])
            if step < left_reach[c]:
                acc[sl, :] += dot(from_right[step, sl, :], u[urows(1 + step), :])
            if step == reach - 1:
                start_tile_gather(c)

    own_rows = pl.ds(pl.multiple_of(t * ra, ra), ra)
    aprime[own_rows, :] = acc[pl.ds(fb, ra), :].astype(jnp.bfloat16)
    for j in range(1, nt):
        go(remote(aprime.at[own_rows], aprime.at[own_rows], a_send.at[j], a_recv.at[j], tdev(j)))

    for c in range(2):
        for j in range(1, nt):
            other = lax.rem(t + (nt - j), nt)
            place = pl.ds(pl.multiple_of(other * fb + c * half, 16), half)
            remote(rin.at[place], rin.at[place], t_send.at[j, c], t_recv.at[j, c], tdev(j)).wait_recv()
    scaled = (dot(vt[...], rin[...]) * inv[...]).astype(jnp.bfloat16)

    outgoing[...] = dot(v[...], scaled).astype(jnp.bfloat16)

    def tile_scatter(j, c):
        owner = lax.rem(t + j, nt)
        src = outgoing.at[pl.ds(pl.multiple_of(owner * fb + c * half, 16), half)]
        return remote(src, arrived.at[j, pl.ds(c * half, half)], s_send.at[j, c], s_recv.at[j, c], tdev(j))

    for c in range(2):
        for j in range(1, nt):
            go(tile_scatter(j, c))

    def scatter_right(step, c):
        sl = pl.ds(c * half, half)
        src = first.at[0, sl] if step == 0 else chain_a.at[step - 1, sl]
        return remote(src, chain_a.at[step, sl], rr_send.at[step, c], rr_recv.at[step, c], zdev(1))

    def scatter_left(step, c):
        sl = pl.ds(c * half, half)
        src = first.at[1, sl] if step == 0 else chain_b.at[step - 1, sl]
        return remote(src, chain_b.at[step, sl], rl_send.at[step, c], rl_recv.at[step, c], zdev(-1))

    def share(c, d):
        return dot_last(rall[a, pl.ds(c * half, half), :], u[urows(d), :])

    for c in range(2):
        sl = pl.ds(c * half, half)
        for j in range(1, nt):
            tile_scatter(j, c).wait_recv()
        total = outgoing[pl.ds(pl.multiple_of(t * fb + c * half, 16), half), :].astype(jnp.float32)
        for j in range(1, nt):
            total += arrived[j, sl, :].astype(jnp.float32)
        rall[a, sl, :] = total.astype(jnp.bfloat16)
        first[0, sl, :] = share(c, right_reach[c]).astype(jnp.bfloat16)
        go(scatter_right(0, c))
        first[1, sl, :] = share(c, -left_reach[c]).astype(jnp.bfloat16)
        go(scatter_left(0, c))

    for j in range(1, na):
        go(remote(rall.at[a], rall.at[a], q_send.at[j], q_recv.at[j], adev(j)))

    def scores():
        for j in range(1, nt):
            other = lax.rem(t + (nt - j), nt)
            place = pl.ds(pl.multiple_of(other * ra, ra), ra)
            remote(aprime.at[place], aprime.at[place], a_send.at[j], a_recv.at[j], tdev(j)).wait_recv()
        for j in range(1, na):
            other = lax.rem(a + (na - j), na)
            remote(rall.at[other], rall.at[other], q_send.at[j], q_recv.at[j], adev(j)).wait_recv()
        position = lax.broadcasted_iota(jnp.int32, (1, nt * ra), 1)
        lane = lax.broadcasted_iota(jnp.int32, (1, 128), 1)
        weights = gt[...].astype(jnp.float32)
        seq_tile[t] = jnp.zeros((8, 128), jnp.float32)
        for q in range(na):
            token = jnp.sum(dot_last(rall[q], aprime[...]) * weights, axis=0, keepdims=True)
            line = jnp.zeros((1, 128), jnp.float32)
            start = jnp.int32(0)
            for s in range(len_ref.shape[1]):
                end = start + len_ref[0, s]
                inside = jnp.logical_and(position >= start, position < end)
                one = jnp.sum(jnp.where(inside, token, 0.0), axis=1, keepdims=True)
                line = jnp.where(lane == s, one, line)
                start = end
            seq_tile[t, pl.ds(q, 1), :] = line
        for j in range(1, nt):
            go(remote(seq_tile.at[t], seq_tile.at[t], pt_send.at[j], pt_recv.at[j], tdev(j)))

    def sum_tile():
        for j in range(1, nt):
            other = lax.rem(t + (nt - j), nt)
            remote(seq_tile.at[other], seq_tile.at[other], pt_send.at[j], pt_recv.at[j], tdev(j)).wait_recv()
        total = seq_tile[0]
        for i in range(1, nt):
            total += seq_tile[i]
        seq_z[z] = total
        for d in range(1, nz):
            go(remote(seq_z.at[z], seq_z.at[z], pz_send.at[d], pz_recv.at[d], zdev(d)))

    def sum_z():
        for d in range(1, nz):
            other = lax.rem(z + (nz - d), nz)
            remote(seq_z.at[other], seq_z.at[other], pz_send.at[d], pz_recv.at[d], zdev(d)).wait_recv()
        total = seq_z[0]
        for i in range(1, nz):
            total += seq_z[i]
        lane = lax.broadcasted_iota(jnp.int32, (1, 128), 1)
        sizes = jnp.ones((1, 128), jnp.float32)
        for s in range(len_ref.shape[1]):
            sizes = jnp.where(lane == s, len_ref[0, s].astype(jnp.float32), sizes)
        score_ref[...] = total / sizes

    for step in range(reach):
        for c in range(2):
            sl = pl.ds(c * half, half)
            if step == 0:
                partial[sl, :] = share(c, 0)
            if step < right_reach[c]:
                left_to_go = right_reach[c] - 1 - step
                if left_to_go > 0:
                    term = share(c, left_to_go)
                    scatter_right(step, c).wait_recv()
                    chain_a[step, sl, :] = (chain_a[step, sl, :].astype(jnp.float32) + term).astype(jnp.bfloat16)
                    go(scatter_right(step + 1, c))
                else:
                    scatter_right(step, c).wait_recv()
                    partial[sl, :] += chain_a[step, sl, :].astype(jnp.float32)
            if step < left_reach[c]:
                left_to_go = left_reach[c] - 1 - step
                if left_to_go > 0:
                    term = share(c, -left_to_go)
                    scatter_left(step, c).wait_recv()
                    chain_b[step, sl, :] = (chain_b[step, sl, :].astype(jnp.float32) + term).astype(jnp.bfloat16)
                    go(scatter_left(step + 1, c))
                else:
                    scatter_left(step, c).wait_recv()
                    partial[sl, :] += chain_b[step, sl, :].astype(jnp.float32)
        if step == reach // 2 - 1:
            scores()
        if step == reach - 3 or (reach < 4 and step == reach - 1):
            sum_tile()
    pre_ref[...] = partial[...].astype(jnp.bfloat16)
    sum_z()
    for copy in sent:
        copy.wait_send()


def per_device(nz, nt, na, query_grads, input_basis, output_basis, eigenvalues, activations, gradients, seq_lengths):
    fb, db = query_grads.shape[1:]
    d_all, f_all = input_basis.shape[0], output_basis.shape[0]
    archive = activations.shape[0]
    ra = archive // nt
    reach = nz // 2
    half = fb // 2
    anywhere = pl.BlockSpec(memory_space=pl.ANY)
    bf16, f32 = jnp.bfloat16, jnp.float32
    dma = pltpu.SemaphoreType.DMA
    pre, scores = pl.pallas_call(
        functools.partial(kernel, nz, nt, na),
        out_shape=(jax.ShapeDtypeStruct((fb, db), bf16), jax.ShapeDtypeStruct((8, 128), f32)),
        in_specs=[anywhere] * 6 + [pl.BlockSpec(memory_space=pltpu.SMEM)],
        out_specs=[pl.BlockSpec(memory_space=pltpu.VMEM)] * 2,
        scratch_shapes=[
            pltpu.VMEM((fb + ra, db), bf16),
            pltpu.VMEM((reach, fb + ra, db), bf16),
            pltpu.VMEM((reach, fb + ra, db), bf16),
            pltpu.VMEM((d_all, db), bf16),
            pltpu.VMEM((fb, f_all), bf16),
            pltpu.VMEM((f_all, fb), bf16),
            pltpu.VMEM((fb, db), f32),
            pltpu.VMEM((fb, archive), bf16),
            pltpu.VMEM((fb + ra, db), f32),
            pltpu.VMEM((f_all, db), bf16),
            pltpu.VMEM((archive, db), bf16),
            pltpu.VMEM((f_all, db), bf16),
            pltpu.VMEM((nt, fb, db), bf16),
            pltpu.VMEM((na, fb, db), bf16),
            pltpu.VMEM((reach, fb, db), bf16),
            pltpu.VMEM((reach, fb, db), bf16),
            pltpu.VMEM((2, fb, db), bf16),
            pltpu.VMEM((fb, db), f32),
            pltpu.VMEM((nt, 8, 128), f32),
            pltpu.VMEM((nz, 8, 128), f32),
            dma((6,)),
            dma((reach, 2)), dma((reach, 2)), dma((reach, 2)), dma((reach, 2)),
            dma((nt, 2)), dma((nt, 2)), dma((nt,)), dma((nt,)), dma((nt, 2)), dma((nt, 2)),
            dma((na,)), dma((na,)),
            dma((reach, 2)), dma((reach, 2)), dma((reach, 2)), dma((reach, 2)),
            dma((nt,)), dma((nt,)), dma((nz,)), dma((nz,)),
        ],
        compiler_params=pltpu.CompilerParams(
            collective_id=0, has_side_effects=True, vmem_limit_bytes=60 * 2**20
        ),
    )(query_grads, input_basis, output_basis.T, eigenvalues, activations, gradients.T, seq_lengths)
    return pre.T[None], scores[:na, : seq_lengths.shape[1]]


def solution(mesh):
    nz, nt, na = mesh.shape["grp"], mesh.shape["tile"], mesh.shape["arch"]
    return jax.shard_map(
        functools.partial(per_device, nz, nt, na),
        mesh=mesh,
        in_specs=(
            P("arch", "tile", "grp"),
            P(None, "grp"),
            P(None, "tile"),
            P("tile", "grp"),
            P("arch", "grp"),
            P("arch", "tile"),
            P("arch", None),
        ),
        out_specs=(P("arch", "grp", "tile"), P(None, "arch")),
        check_vma=False,
    )
```

```python
import functools

import jax
import jax.numpy as jnp
from jax import lax
from jax.experimental import pallas as pl
from jax.experimental.pallas import tpu as pltpu
from jax.sharding import PartitionSpec as P

damping = 0.01
MESH = pl.DeviceIdType.MESH
BF16, F32 = jnp.bfloat16, jnp.float32


def dot(a, b):
    return jnp.dot(a, b, preferred_element_type=F32)


def dot_last(a, b):
    return lax.dot_general(a, b, (((1,), (1,)), ((), ())), preferred_element_type=F32)


def kernel(
    nz, nt, na,
    q_hbm, u_hbm, vt_hbm, eig_hbm, act_hbm, gt_hbm, len_ref,
    pre_ref, score_ref,
    piece, pieces, act, act_right, act_left, u, vt, v, eig, eig_pair, inv, gt,
    acc, acc_act, ybuf, rin, aprime, outgoing, arrived, restored, rall,
    first, chain, final, own, own_pair, seq_tile, seq_z,
    local_sem, f_send, g_send, g_recv, x_send, x_recv,
    ar_send, ar_recv, al_send, al_recv,
    uz_send, uz_recv, ut_send, ut_recv, uc_send, uc_recv,
    e_send, e_recv, t_send, t_recv, a_send, a_recv, s_send, s_recv,
    p_send, p_recv, q_send, q_recv,
    r0_send, r_send, r_recv, rf_recv, o_send, o_recv,
    pt_send, pt_recv, pz_send, pz_recv,
):
    z, t, a = lax.axis_index("grp"), lax.axis_index("tile"), lax.axis_index("arch")
    fb, db = q_hbm.shape[1], q_hbm.shape[2]
    part = fb // 2
    half = part // 2
    ra = act_hbm.shape[0] // nt
    d_all = u_hbm.shape[0]
    up = d_all // (2 * nt)
    reach = nz // 4
    core, pair = lax.rem(a, 2), a - lax.rem(a, 2)
    odd = lax.rem(z, 2)
    mine = pair + odd
    same = lax.rem(z + core, 2) == 0
    other_core = a + 1 - 2 * core
    z_pair = z + 1 - 2 * odd
    chunks = tuple(pl.ds(c * half, half) for c in range(2))

    def at_z(d):
        return lax.rem(z + (d + nz), nz)

    def at_tile(j):
        return lax.rem(t + j, nt)

    def remote(src, dst, send, recv, **dev):
        return pltpu.make_async_remote_copy(
            src_ref=src, dst_ref=dst, send_sem=send, recv_sem=recv, device_id=dev, device_id_type=MESH
        )

    sent = []

    def go(copy):
        copy.start()
        sent.append(copy)

    loads = [
        pltpu.make_async_copy(q_hbm.at[0], piece, local_sem.at[0]),
        pltpu.make_async_copy(act_hbm.at[pl.ds(pl.multiple_of(t * ra, ra), ra)], act, local_sem.at[1]),
        pltpu.make_async_copy(u_hbm, u.at[odd], local_sem.at[2]),
        pltpu.make_async_copy(vt_hbm, vt, local_sem.at[3]),
        pltpu.make_async_copy(eig_hbm, eig, local_sem.at[4]),
        pltpu.make_async_copy(gt_hbm, gt, local_sem.at[5]),
    ]
    for load in loads:
        load.start()

    barrier = pltpu.get_barrier_semaphore()
    peers = [{"grp": at_z(d), "arch": pair + h} for d in (1, -1) for h in (0, 1)]
    peers += [{"grp": at_z(d), "arch": pair + h} for d in (2, -2) for h in (0, 1)]
    peers += [{"tile": at_tile(j), "arch": pair + h} for j in range(1, nt) for h in (0, 1)]
    peers += [{"arch": lax.rem(a + j, na)} for j in range(1, na)]
    for peer in peers:
        pl.semaphore_signal(barrier, inc=1, device_id=peer, device_id_type=MESH)
    for load in loads:
        load.wait()
    pl.semaphore_wait(barrier, len(peers))

    def uz():
        rows = pl.ds(pl.multiple_of((2 * t + core) * up, 128), up)
        return remote(u.at[odd, rows], u.at[odd, rows], uz_send, uz_recv, grp=z_pair)

    def foreign(tile, h):
        return u.at[1 - odd, pl.ds(pl.multiple_of((2 * tile + h) * up, 128), up)]

    def ut(j):
        return remote(foreign(t, core), foreign(t, core), ut_send.at[j], ut_recv.at[j], tile=at_tile(j))

    def uc(j):
        rows = foreign(at_tile(nt - j), core)
        return remote(rows, rows, uc_send.at[j], uc_recv.at[j], arch=other_core)

    go(uz())

    hop = 2 - lax.rem(z + core, 2)
    for c in range(2):
        for h in range(2):
            src = piece.at[pl.ds(h * part + c * half, half)]
            for side, (to, slot) in enumerate(((lax.rem(z + hop, nz), nz - hop), (lax.rem(z + nz - hop, nz), hop))):
                go(remote(
                    src, pieces.at[slot, chunks[c]], f_send.at[side, h, c], g_recv.at[slot, c], grp=to, arch=pair + h
                ))

    def from_core():
        rows = pl.ds(pl.multiple_of((1 - core) * part, 16), part)
        return remote(piece.at[rows], pieces.at[0], x_send, x_recv, arch=other_core)

    @pl.when(same)
    def _():
        from_core().start()
        pieces[0] = piece[pl.ds(pl.multiple_of(core * part, 16), part), :]

    def act_hop(step, side):
        buf, send, recv, d = ((act_right, ar_send, ar_recv, 1), (act_left, al_send, al_recv, -1))[side]
        src = act if step == 0 else buf.at[step - 1]
        return remote(src, buf.at[step], send.at[step], recv.at[step], grp=at_z(d))

    act_reach = (nz // 2, nz // 2 - 1)
    go(act_hop(0, 0))
    go(act_hop(0, 1))

    def urows(d):
        return pl.ds(pl.multiple_of(at_z(d) * db, 128), db)

    def act_step(step):
        for side in range(2):
            if step < act_reach[side]:
                act_hop(step, side).wait_recv()
                if step + 1 < act_reach[side]:
                    go(act_hop(step + 1, side))
        for side, (buf, d) in enumerate(((act_right, -1 - step), (act_left, 1 + step))):
            if step < act_reach[side]:
                acc_act[...] += dot(buf[step], u[odd, urows(d), :])

    def arrive(slot, c):
        remote(piece.at[chunks[c]], pieces.at[slot, chunks[c]], g_send.at[slot, c], g_recv.at[slot, c], grp=z).wait_recv()

    def forward(slot, c, d):
        to = (slot - d) % nz
        go(remote(
            pieces.at[slot, chunks[c]], pieces.at[to, chunks[c]], g_send.at[to, c], g_recv.at[to, c], grp=at_z(d)
        ))

    acc_act[...] = dot(act[...], u[odd, urows(0), :])
    v[...] = vt[...].T

    @pl.when(jnp.logical_not(same))
    def _():
        from_core().wait_recv()

    acc[odd] = dot(pieces[0], u[odd, urows(0), :])
    ready, act_at = [0], 0
    per_step = -(-(nz // 2 - 2) // reach)
    for step in range(reach):
        new = []
        if step == reach - 1:
            for j in range(nt):
                if j:
                    ut_from = foreign(at_tile(nt - j), core)
                    remote(ut_from, ut_from, ut_send.at[j], ut_recv.at[j], tile=at_tile(j)).wait_recv()
                go(uc(j))

            @pl.when(same)
            def _():
                remote(eig, eig_pair, e_send, e_recv, grp=z_pair).start()

        for c in range(2):
            for far in (0, 1):
                for side, d in enumerate((2, -2)):
                    last = reach if far else reach - (c != side)
                    if step >= last:
                        continue
                    dist = 2 * step + (1 if far else 2)
                    slot = (-dist if side == 0 else dist) % nz
                    arrive(slot, c)
                    if step + 1 < last:
                        forward(slot, c, d)
                    if slot not in new:
                        new.append(slot)
        if step == reach - 1:
            for j in range(nt):
                rows = foreign(at_tile(nt - j), 1 - core)
                remote(rows, rows, uc_send.at[j], uc_recv.at[j], arch=other_core).wait_recv()
        else:
            if step == 0:
                uz_rows = foreign(t, core)
                remote(uz_rows, uz_rows, uz_send, uz_recv, grp=z_pair).wait_recv()
                for j in range(1, nt):
                    go(ut(j))
        for slot in new:
            acc[odd] += dot(pieces[slot], u[odd, urows(slot), :])
        ready += new
        if step < reach - 1:
            for _ in range(per_step if step else 1):
                if act_at < nz // 2 - 2:
                    act_step(act_at)
                    act_at += 1
    total = dot(pieces[0], u[1 - odd, urows(0), :])
    for slot in ready[1:]:
        total += dot(pieces[slot], u[1 - odd, urows(slot), :])
    ybuf[1 - odd] = total.astype(BF16)
    ybuf[odd] = acc[odd].astype(BF16)

    def rin_rows(tile, h):
        return pl.ds(pl.multiple_of(tile * fb + h * part, 16), part)

    def tile_gather(j, e):
        rows = rin.at[rin_rows(t, core)]
        return remote(
            ybuf.at[e], rows, t_send.at[j, e], t_recv.at[j, core], tile=at_tile(j), arch=pair + e
        )

    for j in range(1, nt):
        for e in range(2):
            go(tile_gather(j, e))
    cross = remote(
        ybuf.at[1 - core], rin.at[rin_rows(t, core)], t_send.at[0, 0], t_recv.at[0, core], arch=other_core
    )
    go(cross)
    rin[rin_rows(t, core), :] = ybuf[core]
    for step in range(act_at, nz // 2):
        act_step(step)
    own_rows = pl.ds(pl.multiple_of(t * ra, ra), ra)
    aprime[own_rows, :] = acc_act[...].astype(BF16)

    @pl.when(jnp.logical_not(same))
    def _():
        remote(eig, eig_pair, e_send, e_recv, grp=z_pair).wait_recv()
        inv[...] = 1.0 / (eig_pair[...] + damping)

    @pl.when(same)
    def _():
        inv[...] = 1.0 / (eig[...] + damping)

    def tile_wait(j, h):
        rows = rin.at[rin_rows(at_tile(nt - j), h)]
        remote(rows, rows, t_send.at[j, 0], t_recv.at[j, h], arch=other_core).wait_recv()

    tile_wait(0, 1 - core)
    for j in range(1, nt):
        for h in range(2):
            tile_wait(j, h)
    scaled = (dot(vt[...], rin[...]) * inv[...]).astype(BF16)

    outgoing[...] = dot(v[...], scaled).astype(BF16)

    def tile_scatter(j, h):
        src = outgoing.at[rin_rows(at_tile(j), h)]
        return remote(src, arrived.at[j, core], s_send.at[j, h], s_recv.at[j, core], tile=at_tile(j), arch=pair + h)

    for j in range(1, nt):
        for h in range(2):
            go(tile_scatter(j, h))
    go(remote(
        outgoing.at[rin_rows(t, 1 - core)], arrived.at[0, core], s_send.at[0, 0], s_recv.at[0, core], arch=other_core
    ))
    arrived[0, core] = outgoing[rin_rows(t, core), :]
    for j in range(1, nt):
        go(remote(aprime.at[own_rows], aprime.at[own_rows], a_send.at[j], a_recv.at[j], tile=at_tile(j)))

    def scatter_wait(j, e):
        dst = arrived.at[j, e]
        remote(dst, dst, s_send.at[j, 0], s_recv.at[j, e], arch=other_core).wait_recv()

    scatter_wait(0, 1 - core)
    for j in range(1, nt):
        for e in range(2):
            scatter_wait(j, e)
    for e in range(2):
        total = arrived[0, e].astype(F32)
        for j in range(1, nt):
            total += arrived[j, e].astype(F32)
        restored[e] = total.astype(BF16)

    def share(d):
        rows = urows(d)
        return dot_last(restored[0], u[0, rows, :]) + dot_last(restored[1], u[1, rows, :])

    def lasts(far, side):
        return tuple(reach if far else reach - (c != side) for c in range(2))

    def scatter(step, c, far, side):
        last = lasts(far, side)[c]
        src = first.at[far, side, chunks[c]] if step == 0 else chain.at[far, side, step - 1, chunks[c]]
        d = 2 if side == 0 else -2
        if step < last - 1:
            return remote(
                src, chain.at[far, side, step, chunks[c]], r_send.at[far, side, step, c],
                r_recv.at[far, side, step, c], grp=at_z(d),
            )
        return remote(
            src, final.at[side, core, chunks[c]], r0_send.at[far, side, c], rf_recv.at[side, core, c],
            grp=at_z(d // 2 if far else d), arch=mine,
        )

    def distance(step, c, far, side):
        m = 2 * (lasts(far, side)[c] - step) - far
        return m if side == 0 else -m

    for far in (0, 1):
        for side in range(2):
            terms = {}
            for c in range(2):
                m = distance(0, c, far, side)
                if m not in terms:
                    terms[m] = share(m)
                first[far, side, chunks[c], :] = terms[m][c * half:(c + 1) * half].astype(BF16)
                go(scatter(0, c, far, side))

    core_rows = pl.ds(pl.multiple_of(core * part, 16), part)
    rall[mine, core_rows, :] = restored[odd]
    go(remote(restored.at[1 - odd], rall.at[mine, core_rows], p_send, p_recv, grp=z_pair))
    for j in range(1, na):
        go(remote(
            rall.at[mine, core_rows], rall.at[mine, core_rows], q_send.at[j, 0], q_recv.at[j, 0], arch=lax.rem(a + j, na)
        ))

    def spread():
        slot = rall.at[pair + 1 - odd, core_rows]
        remote(slot, slot, p_send, p_recv, grp=z_pair).wait_recv()
        for j in range(1, na):
            go(remote(slot, slot, q_send.at[j, 1], q_recv.at[j, 1], arch=lax.rem(a + j, na)))

    def scores():
        for j in range(1, nt):
            place = aprime.at[pl.ds(pl.multiple_of(at_tile(nt - j) * ra, ra), ra)]
            remote(place, place, a_send.at[j], a_recv.at[j], tile=at_tile(j)).wait_recv()
        for j in range(1, na):
            src = lax.rem(a + (na - j), na)
            src_core = lax.rem(src, 2)
            rows = pl.ds(pl.multiple_of(src_core * part, 16), part)
            for which, q in enumerate((src - src_core + odd, src - src_core + 1 - odd)):
                slot = rall.at[q, rows]
                remote(slot, slot, q_send.at[j, which], q_recv.at[j, which], arch=src).wait_recv()
        position = lax.broadcasted_iota(jnp.int32, (1, nt * ra), 1)
        lane = lax.broadcasted_iota(jnp.int32, (1, 128), 1)
        weights = gt[...].astype(F32)
        seq_tile[t] = jnp.zeros((8, 128), F32)
        for q in range(na):
            token = jnp.sum(dot_last(rall[q], aprime[...]) * weights, axis=0, keepdims=True)
            line = jnp.zeros((1, 128), F32)
            start = jnp.int32(0)
            for s in range(len_ref.shape[1]):
                end = start + len_ref[0, s]
                inside = jnp.logical_and(position >= start, position < end)
                one = jnp.sum(jnp.where(inside, token, 0.0), axis=1, keepdims=True)
                line = jnp.where(lane == s, one, line)
                start = end
            seq_tile[t, pl.ds(q, 1), :] = line
        for j in range(1, nt):
            go(remote(seq_tile.at[t], seq_tile.at[t], pt_send.at[j], pt_recv.at[j], tile=at_tile(j)))

    def sum_tile():
        for j in range(1, nt):
            slot = seq_tile.at[at_tile(nt - j)]
            remote(slot, slot, pt_send.at[j], pt_recv.at[j], tile=at_tile(j)).wait_recv()
        total = seq_tile[0]
        for i in range(1, nt):
            total += seq_tile[i]
        seq_z[z] = total
        for d in range(1, nz):
            go(remote(seq_z.at[z], seq_z.at[z], pz_send.at[d], pz_recv.at[d], grp=at_z(d)))

    def sum_z():
        for d in range(1, nz):
            slot = seq_z.at[at_z(-d)]
            remote(slot, slot, pz_send.at[d], pz_recv.at[d], grp=at_z(d)).wait_recv()
        total = seq_z[0]
        for i in range(1, nz):
            total += seq_z[i]
        lane = lax.broadcasted_iota(jnp.int32, (1, 128), 1)
        sizes = jnp.ones((1, 128), F32)
        for s in range(len_ref.shape[1]):
            sizes = jnp.where(lane == s, len_ref[0, s].astype(F32), sizes)
        score_ref[...] = total / sizes

    for step in range(1, reach):
        for far in (0, 1):
            for side in range(2):
                terms = {}
                for c in range(2):
                    if step < lasts(far, side)[c]:
                        m = distance(step, c, far, side)
                        if m not in terms:
                            terms[m] = share(m)
                for c in range(2):
                    if step >= lasts(far, side)[c]:
                        continue
                    m = distance(step, c, far, side)
                    scatter(step - 1, c, far, side).wait_recv()
                    got = chain[far, side, step - 1, chunks[c], :].astype(F32)
                    chain[far, side, step - 1, chunks[c], :] = (
                        got + terms[m][c * half:(c + 1) * half]
                    ).astype(BF16)
                    go(scatter(step, c, far, side))
        if step == 1:
            own[...] = share(0)

            @pl.when(jnp.logical_not(same))
            def _():
                own_pair[0] = own[...].astype(BF16)
                remote(own_pair.at[0], own_pair.at[1], o_send, o_recv, arch=other_core).start()

            spread()
        if step == max(reach - 2, 1):
            scores()
        if step == reach - 1:
            sum_tile()

    for side in range(2):
        for h in range(2):
            for c in range(2):
                slot = final.at[side, h, chunks[c]]
                remote(slot, slot, r0_send.at[0, side, c], rf_recv.at[side, h, c], grp=z_pair).wait_recv()
    for h in range(2):
        total = final[0, h].astype(F32) + final[1, h].astype(F32)
        pre_ref[pl.ds(h * part, part), :] = total.astype(BF16)

    @pl.when(same)
    def _():
        remote(own_pair.at[0], own_pair.at[1], o_send, o_recv, arch=other_core).wait_recv()
        for h, term in ((core, own[...]), (1 - core, own_pair[1].astype(F32))):
            total = final[0, h].astype(F32) + final[1, h].astype(F32) + term
            pre_ref[pl.ds(pl.multiple_of(h * part, 16), part), :] = total.astype(BF16)

    sum_z()
    for copy in sent:
        copy.wait_send()

    @pl.when(same)
    def _():
        from_core().wait_send()
        remote(eig, eig_pair, e_send, e_recv, grp=z_pair).wait_send()

    @pl.when(jnp.logical_not(same))
    def _():
        remote(own_pair.at[0], own_pair.at[1], o_send, o_recv, arch=other_core).wait_send()


def per_device(nz, nt, na, query_grads, input_basis, output_basis, eigenvalues, activations, gradients, seq_lengths):
    fb, db = query_grads.shape[1:]
    d_all, f_all = input_basis.shape[0], output_basis.shape[0]
    archive = activations.shape[0]
    ra = archive // nt
    part = fb // 2
    reach = nz // 4
    anywhere = pl.BlockSpec(memory_space=pl.ANY)
    dma = pltpu.SemaphoreType.DMA
    vmem = pltpu.VMEM
    one = dma(())
    pre, scores = pl.pallas_call(
        functools.partial(kernel, nz, nt, na),
        out_shape=(jax.ShapeDtypeStruct((fb, db), BF16), jax.ShapeDtypeStruct((8, 128), F32)),
        in_specs=[anywhere] * 6 + [pl.BlockSpec(memory_space=pltpu.SMEM)],
        out_specs=[pl.BlockSpec(memory_space=pltpu.VMEM)] * 2,
        scratch_shapes=[
            vmem((fb, db), BF16),
            vmem((nz, part, db), BF16),
            vmem((ra, db), BF16),
            vmem((nz // 2, ra, db), BF16),
            vmem((nz // 2, ra, db), BF16),
            vmem((2, d_all, db), BF16),
            vmem((fb, f_all), BF16),
            vmem((f_all, fb), BF16),
            vmem((fb, db), F32),
            vmem((fb, db), F32),
            vmem((fb, db), F32),
            vmem((fb, archive), BF16),
            vmem((2, part, db), F32),
            vmem((ra, db), F32),
            vmem((2, part, db), BF16),
            vmem((f_all, db), BF16),
            vmem((archive, db), BF16),
            vmem((f_all, db), BF16),
            vmem((nt, 2, part, db), BF16),
            vmem((2, part, db), BF16),
            vmem((na, fb, db), BF16),
            vmem((2, 2, part, db), BF16),
            vmem((2, 2, reach, part, db), BF16),
            vmem((2, 2, part, db), BF16),
            vmem((part, db), F32),
            vmem((2, part, db), BF16),
            vmem((nt, 8, 128), F32),
            vmem((nz, 8, 128), F32),
            dma((6,)), dma((2, 2, 2)), dma((nz, 2)), dma((nz, 2)), one, one,
            dma((nz // 2,)), dma((nz // 2,)), dma((nz // 2,)), dma((nz // 2,)),
            one, one, dma((nt,)), dma((nt,)), dma((nt,)), dma((nt,)),
            one, one, dma((nt, 2)), dma((nt, 2)), dma((nt,)), dma((nt,)), dma((nt, 2)), dma((nt, 2)),
            one, one, dma((na, 2)), dma((na, 2)),
            dma((2, 2, 2)), dma((2, 2, reach, 2)), dma((2, 2, reach, 2)), dma((2, 2, 2)), one, one,
            dma((nt,)), dma((nt,)), dma((nz,)), dma((nz,)),
        ],
        compiler_params=pltpu.CompilerParams(
            collective_id=0, has_side_effects=True, vmem_limit_bytes=60 * 2**20
        ),
    )(query_grads, input_basis, output_basis.T, eigenvalues, activations, gradients.T, seq_lengths)
    return pre.T[None], scores[:na, : seq_lengths.shape[1]]


def solution(mesh):
    nz, nt, na = mesh.shape["grp"], mesh.shape["tile"], mesh.shape["arch"]
    return jax.shard_map(
        functools.partial(per_device, nz, nt, na),
        mesh=mesh,
        in_specs=(
            P("arch", "tile", "grp"),
            P(None, "grp"),
            P(None, "tile"),
            P("tile", "grp"),
            P("arch", "grp"),
            P("arch", "tile"),
            P("arch", None),
        ),
        out_specs=(P("arch", "grp", "tile"), P(None, "arch")),
        check_vma=False,
    )
```

```python
import functools

import jax
import jax.numpy as jnp
from jax import lax
from jax.experimental import pallas as pl
from jax.experimental.pallas import tpu as pltpu
from jax.sharding import PartitionSpec as P

damping = 0.01
MESH = pl.DeviceIdType.MESH
BF16, F32 = jnp.bfloat16, jnp.float32


def dot(a, b):
    return jnp.dot(a, b, preferred_element_type=F32)


def dot_last(a, b):
    return lax.dot_general(a, b, (((1,), (1,)), ((), ())), preferred_element_type=F32)


def kernel(
    nz, nt, na,
    q_hbm, u_hbm, vt_hbm, eig_hbm, act_hbm, gt_hbm, len_ref,
    pre_ref, score_ref,
    piece, pieces, act, acts, u, vt, v, eig, eig_pair, inv, gt,
    acc, ybuf, rin, aprime, outgoing, arrived, restored, rall,
    first, chain, final, own, own_pair, tokens, seq_tile, seq_z,
    local_sem, f_send, g_send, g_recv, x_send, x_recv,
    ar_send, ar_recv,
    uz_send, uz_recv, ut_send, ut_recv, uc_send, uc_recv,
    e_send, e_recv, t_send, t_recv, a_send, a_recv, s_send, s_recv,
    p_send, p_recv, q_send, q_recv,
    r0_send, r_send, r_recv, rf_recv, o_send, o_recv,
    pt_send, pt_recv, pz_send, pz_recv,
):
    z, t, a = lax.axis_index("grp"), lax.axis_index("tile"), lax.axis_index("arch")
    fb, db = q_hbm.shape[1], q_hbm.shape[2]
    part = fb // 2
    half = part // 2
    ra = act_hbm.shape[0] // nt
    d_all = u_hbm.shape[0]
    up = d_all // (2 * nt)
    reach = nz // 4
    core, pair = lax.rem(a, 2), a - lax.rem(a, 2)
    odd = lax.rem(z, 2)
    mine = pair + odd
    same = lax.rem(z + core, 2) == 0
    other_core = a + 1 - 2 * core
    z_pair = z + 1 - 2 * odd
    chunks = tuple(pl.ds(c * half, half) for c in range(2))

    def at_z(d):
        return lax.rem(z + (d + nz), nz)

    def at_tile(j):
        return lax.rem(t + j, nt)

    def remote(src, dst, send, recv, **dev):
        return pltpu.make_async_remote_copy(
            src_ref=src, dst_ref=dst, send_sem=send, recv_sem=recv, device_id=dev, device_id_type=MESH
        )

    sent = []

    def go(copy):
        copy.start()
        sent.append(copy)

    loads = [
        pltpu.make_async_copy(q_hbm.at[0], piece, local_sem.at[0]),
        pltpu.make_async_copy(act_hbm.at[pl.ds(pl.multiple_of(t * ra, ra), ra)], act, local_sem.at[1]),
        pltpu.make_async_copy(u_hbm, u.at[odd], local_sem.at[2]),
        pltpu.make_async_copy(vt_hbm, vt, local_sem.at[3]),
        pltpu.make_async_copy(eig_hbm, eig, local_sem.at[4]),
        pltpu.make_async_copy(gt_hbm, gt, local_sem.at[5]),
    ]
    for load in loads:
        load.start()

    barrier = pltpu.get_barrier_semaphore()
    peers = [{"grp": at_z(d), "arch": pair + h} for d in (1, -1) for h in (0, 1)]
    peers += [{"grp": at_z(d), "arch": pair + h} for d in (2, -2) for h in (0, 1)]
    peers += [{"tile": at_tile(j), "arch": pair + h} for j in range(1, nt) for h in (0, 1)]
    peers += [{"arch": lax.rem(a + j, na)} for j in range(1, na)]
    for peer in peers:
        pl.semaphore_signal(barrier, inc=1, device_id=peer, device_id_type=MESH)
    loads[0].wait()
    pl.semaphore_wait(barrier, len(peers))

    def uz():
        rows = pl.ds(pl.multiple_of((2 * t + core) * up, 128), up)
        return remote(u.at[odd, rows], u.at[odd, rows], uz_send, uz_recv, grp=z_pair)

    def foreign(tile, h):
        return u.at[1 - odd, pl.ds(pl.multiple_of((2 * tile + h) * up, 128), up)]

    def ut(j):
        return remote(foreign(t, core), foreign(t, core), ut_send.at[j], ut_recv.at[j], tile=at_tile(j))

    def uc(j):
        rows = foreign(at_tile(nt - j), core)
        return remote(rows, rows, uc_send.at[j], uc_recv.at[j], arch=other_core)

    hop = 2 - lax.rem(z + core, 2)
    for c in range(2):
        for h in range(2):
            src = piece.at[pl.ds(h * part + c * half, half)]
            for side, (to, slot) in enumerate(((lax.rem(z + hop, nz), nz - hop), (lax.rem(z + nz - hop, nz), hop))):
                go(remote(
                    src, pieces.at[slot, chunks[c]], f_send.at[side, h, c], g_recv.at[slot, c], grp=to, arch=pair + h
                ))

    def from_core():
        rows = pl.ds(pl.multiple_of((1 - core) * part, 16), part)
        return remote(piece.at[rows], pieces.at[0], x_send, x_recv, arch=other_core)

    @pl.when(same)
    def _():
        from_core().start()
        pieces[0] = piece[pl.ds(pl.multiple_of(core * part, 16), part), :]

    loads[2].wait()
    go(uz())
    for load in (loads[1], *loads[3:]):
        load.wait()

    def urows(d):
        return pl.ds(pl.multiple_of(at_z(d) * db, 128), db)

    own_rows = pl.ds(pl.multiple_of(t * ra, ra), ra)

    def act_product():
        total = dot(act[...], u[odd, urows(0), :])
        for d in range(1, nz):
            remote(act, acts.at[d], ar_send.at[d], ar_recv.at[d], grp=at_z(d)).wait_recv()
            total += dot(acts[d], u[odd, urows(-d), :])
        aprime[own_rows, :] = total.astype(BF16)
        for j in range(1, nt):
            go(remote(aprime.at[own_rows], aprime.at[own_rows], a_send.at[j], a_recv.at[j], tile=at_tile(j)))

    def arrive(slot, c):
        remote(piece.at[chunks[c]], pieces.at[slot, chunks[c]], g_send.at[slot, c], g_recv.at[slot, c], grp=z).wait_recv()

    def forward(slot, c, d):
        to = (slot - d) % nz
        go(remote(
            pieces.at[slot, chunks[c]], pieces.at[to, chunks[c]], g_send.at[to, c], g_recv.at[to, c], grp=at_z(d)
        ))

    v[...] = vt[...].T

    @pl.when(jnp.logical_not(same))
    def _():
        from_core().wait_recv()

    acc[odd] = dot(pieces[0], u[odd, urows(0), :])
    ready = [0]
    for step in range(reach):
        new = []
        if step == reach - 1:
            for j in range(nt):
                if j:
                    ut_from = foreign(at_tile(nt - j), core)
                    remote(ut_from, ut_from, ut_send.at[j], ut_recv.at[j], tile=at_tile(j)).wait_recv()
                go(uc(j))

            @pl.when(same)
            def _():
                remote(eig, eig_pair, e_send, e_recv, grp=z_pair).start()

        for c in range(2):
            for far in (0, 1):
                for side, d in enumerate((2, -2)):
                    last = reach if far else reach - (c != side)
                    if step >= last:
                        continue
                    dist = 2 * step + (1 if far else 2)
                    slot = (-dist if side == 0 else dist) % nz
                    arrive(slot, c)
                    if step + 1 < last:
                        forward(slot, c, d)
                    if slot not in new:
                        new.append(slot)
        if step == reach - 1:
            for j in range(nt):
                rows = foreign(at_tile(nt - j), 1 - core)
                remote(rows, rows, uc_send.at[j], uc_recv.at[j], arch=other_core).wait_recv()
        else:
            if step == 0:
                uz_rows = foreign(t, core)
                remote(uz_rows, uz_rows, uz_send, uz_recv, grp=z_pair).wait_recv()
                for j in range(1, nt):
                    go(ut(j))
        for slot in new:
            acc[odd] += dot(pieces[slot], u[odd, urows(slot), :])
        ready += new
    total = dot(pieces[0], u[1 - odd, urows(0), :])
    for slot in ready[1:]:
        total += dot(pieces[slot], u[1 - odd, urows(slot), :])
    ybuf[1 - odd] = total.astype(BF16)
    ybuf[odd] = acc[odd].astype(BF16)

    def rin_rows(tile, h):
        return pl.ds(pl.multiple_of(tile * fb + h * part, 16), part)

    def tile_gather(j, e):
        rows = rin.at[rin_rows(t, core)]
        return remote(
            ybuf.at[e], rows, t_send.at[j, e], t_recv.at[j, core], tile=at_tile(j), arch=pair + e
        )

    for j in range(1, nt):
        for e in range(2):
            go(tile_gather(j, e))
    cross = remote(
        ybuf.at[1 - core], rin.at[rin_rows(t, core)], t_send.at[0, 0], t_recv.at[0, core], arch=other_core
    )
    go(cross)
    rin[rin_rows(t, core), :] = ybuf[core]
    for d in sorted(range(1, nz), key=lambda k: -min(k, nz - k)):
        go(remote(act, acts.at[d], ar_send.at[d], ar_recv.at[d], grp=at_z(d)))

    @pl.when(jnp.logical_not(same))
    def _():
        remote(eig, eig_pair, e_send, e_recv, grp=z_pair).wait_recv()
        inv[...] = 1.0 / (eig_pair[...] + damping)

    @pl.when(same)
    def _():
        inv[...] = 1.0 / (eig[...] + damping)

    def tile_wait(j, h):
        rows = rin.at[rin_rows(at_tile(nt - j), h)]
        remote(rows, rows, t_send.at[j, 0], t_recv.at[j, h], arch=other_core).wait_recv()

    tile_wait(0, 1 - core)
    for j in range(1, nt):
        for h in range(2):
            tile_wait(j, h)
    scaled = (dot(vt[...], rin[...]) * inv[...]).astype(BF16)

    outgoing[...] = dot(v[...], scaled).astype(BF16)

    def tile_scatter(j, h):
        src = outgoing.at[rin_rows(at_tile(j), h)]
        return remote(src, arrived.at[j, core], s_send.at[j, h], s_recv.at[j, core], tile=at_tile(j), arch=pair + h)

    for j in range(1, nt):
        for h in range(2):
            go(tile_scatter(j, h))
    go(remote(
        outgoing.at[rin_rows(t, 1 - core)], arrived.at[0, core], s_send.at[0, 0], s_recv.at[0, core], arch=other_core
    ))
    arrived[0, core] = outgoing[rin_rows(t, core), :]

    def scatter_wait(j, e):
        dst = arrived.at[j, e]
        remote(dst, dst, s_send.at[j, 0], s_recv.at[j, e], arch=other_core).wait_recv()

    scatter_wait(0, 1 - core)
    for j in range(1, nt):
        for e in range(2):
            scatter_wait(j, e)
    for e in range(2):
        total = arrived[0, e].astype(F32)
        for j in range(1, nt):
            total += arrived[j, e].astype(F32)
        restored[e] = total.astype(BF16)

    def share(d):
        rows = urows(d)
        return dot_last(restored[0], u[0, rows, :]) + dot_last(restored[1], u[1, rows, :])

    def lasts(far, side):
        return tuple(reach if far else reach - (c != side) for c in range(2))

    def scatter(step, c, far, side):
        last = lasts(far, side)[c]
        src = first.at[far, side, chunks[c]] if step == 0 else chain.at[far, side, step - 1, chunks[c]]
        d = 2 if side == 0 else -2
        if step < last - 1:
            return remote(
                src, chain.at[far, side, step, chunks[c]], r_send.at[far, side, step, c],
                r_recv.at[far, side, step, c], grp=at_z(d),
            )
        return remote(
            src, final.at[side, core, chunks[c]], r0_send.at[far, side, c], rf_recv.at[side, core, c],
            grp=at_z(d // 2 if far else d), arch=mine,
        )

    def distance(step, c, far, side):
        m = 2 * (lasts(far, side)[c] - step) - far
        return m if side == 0 else -m

    core_rows = pl.ds(pl.multiple_of(core * part, 16), part)
    rall[mine, core_rows, :] = restored[odd]
    go(remote(restored.at[1 - odd], rall.at[mine, core_rows], p_send, p_recv, grp=z_pair))
    for j in range(1, na):
        go(remote(
            rall.at[mine, core_rows], rall.at[mine, core_rows], q_send.at[j, 0], q_recv.at[j, 0], arch=lax.rem(a + j, na)
        ))

    for far in (0, 1):
        for side in range(2):
            terms = {}
            for c in range(2):
                m = distance(0, c, far, side)
                if m not in terms:
                    terms[m] = share(m)
                first[far, side, chunks[c], :] = terms[m][c * half:(c + 1) * half].astype(BF16)
                go(scatter(0, c, far, side))

    act_product()

    def spread():
        slot = rall.at[pair + 1 - odd, core_rows]
        remote(slot, slot, p_send, p_recv, grp=z_pair).wait_recv()
        for j in range(1, na):
            go(remote(slot, slot, q_send.at[j, 1], q_recv.at[j, 1], arch=lax.rem(a + j, na)))

    def token(q):
        product = dot_last(rall[q], aprime[...]) * gt[...].astype(F32)
        tokens[pl.ds(q, 1), :] = jnp.sum(product, axis=0, keepdims=True)

    def arch_wait(which):
        for j in range(1, na):
            src = lax.rem(a + (na - j), na)
            src_core = lax.rem(src, 2)
            q = src - src_core + (odd if which == 0 else 1 - odd)
            slot = rall.at[q, pl.ds(pl.multiple_of(src_core * part, 16), part)]
            remote(slot, slot, q_send.at[j, which], q_recv.at[j, which], arch=src).wait_recv()

    def scores():
        position = lax.broadcasted_iota(jnp.int32, (8, nt * ra), 1)
        lane = lax.broadcasted_iota(jnp.int32, (8, 128), 1)
        line = jnp.zeros((8, 128), F32)
        start = jnp.int32(0)
        for s in range(len_ref.shape[1]):
            end = start + len_ref[0, s]
            inside = jnp.logical_and(position >= start, position < end)
            one = jnp.sum(jnp.where(inside, tokens[...], 0.0), axis=1, keepdims=True)
            line = jnp.where(lane == s, one, line)
            start = end
        seq_tile[t] = line
        for j in range(1, nt):
            go(remote(seq_tile.at[t], seq_tile.at[t], pt_send.at[j], pt_recv.at[j], tile=at_tile(j)))

    def sum_tile():
        for j in range(1, nt):
            slot = seq_tile.at[at_tile(nt - j)]
            remote(slot, slot, pt_send.at[j], pt_recv.at[j], tile=at_tile(j)).wait_recv()
        total = seq_tile[0]
        for i in range(1, nt):
            total += seq_tile[i]
        seq_z[z] = total
        for d in range(1, nz):
            go(remote(seq_z.at[z], seq_z.at[z], pz_send.at[d], pz_recv.at[d], grp=at_z(d)))

    def sum_z():
        for d in range(1, nz):
            slot = seq_z.at[at_z(-d)]
            remote(slot, slot, pz_send.at[d], pz_recv.at[d], grp=at_z(d)).wait_recv()
        total = seq_z[0]
        for i in range(1, nz):
            total += seq_z[i]
        lane = lax.broadcasted_iota(jnp.int32, (1, 128), 1)
        sizes = jnp.ones((1, 128), F32)
        for s in range(len_ref.shape[1]):
            sizes = jnp.where(lane == s, len_ref[0, s].astype(F32), sizes)
        score_ref[...] = total / sizes

    spread()
    for step in range(1, reach):
        for far in (0, 1):
            for side in range(2):
                terms = {}
                for c in range(2):
                    if step < lasts(far, side)[c]:
                        m = distance(step, c, far, side)
                        if m not in terms:
                            terms[m] = share(m)
                for c in range(2):
                    if step >= lasts(far, side)[c]:
                        continue
                    m = distance(step, c, far, side)
                    scatter(step - 1, c, far, side).wait_recv()
                    got = chain[far, side, step - 1, chunks[c], :].astype(F32)
                    chain[far, side, step - 1, chunks[c], :] = (
                        got + terms[m][c * half:(c + 1) * half]
                    ).astype(BF16)
                    go(scatter(step, c, far, side))
        if step == 1:
            own[...] = share(0)

            @pl.when(jnp.logical_not(same))
            def _():
                own_pair[0] = own[...].astype(BF16)
                remote(own_pair.at[0], own_pair.at[1], o_send, o_recv, arch=other_core).start()

            tokens[...] = jnp.zeros_like(tokens)
            for j in range(1, nt):
                place = aprime.at[pl.ds(pl.multiple_of(at_tile(nt - j) * ra, ra), ra)]
                remote(place, place, a_send.at[j], a_recv.at[j], tile=at_tile(j)).wait_recv()
            for which in range(2):
                arch_wait(which)
                q = odd if which == 0 else 1 - odd
                token(q)
                token(2 + q)
            scores()
        if step == max(reach - 2, 2):
            sum_tile()

    if reach == 2:
        sum_tile()
    for side in range(2):
        for h in range(2):
            for c in range(2):
                slot = final.at[side, h, chunks[c]]
                remote(slot, slot, r0_send.at[0, side, c], rf_recv.at[side, h, c], grp=z_pair).wait_recv()
    for h in range(2):
        total = final[0, h].astype(F32) + final[1, h].astype(F32)
        pre_ref[pl.ds(h * part, part), :] = total.astype(BF16)

    @pl.when(same)
    def _():
        remote(own_pair.at[0], own_pair.at[1], o_send, o_recv, arch=other_core).wait_recv()
        for h, term in ((core, own[...]), (1 - core, own_pair[1].astype(F32))):
            total = final[0, h].astype(F32) + final[1, h].astype(F32) + term
            pre_ref[pl.ds(pl.multiple_of(h * part, 16), part), :] = total.astype(BF16)

    sum_z()
    for copy in sent:
        copy.wait_send()

    @pl.when(same)
    def _():
        from_core().wait_send()
        remote(eig, eig_pair, e_send, e_recv, grp=z_pair).wait_send()

    @pl.when(jnp.logical_not(same))
    def _():
        remote(own_pair.at[0], own_pair.at[1], o_send, o_recv, arch=other_core).wait_send()


def per_device(nz, nt, na, query_grads, input_basis, output_basis, eigenvalues, activations, gradients, seq_lengths):
    fb, db = query_grads.shape[1:]
    d_all, f_all = input_basis.shape[0], output_basis.shape[0]
    archive = activations.shape[0]
    ra = archive // nt
    part = fb // 2
    reach = nz // 4
    anywhere = pl.BlockSpec(memory_space=pl.ANY)
    dma = pltpu.SemaphoreType.DMA
    vmem = pltpu.VMEM
    one = dma(())
    pre, scores = pl.pallas_call(
        functools.partial(kernel, nz, nt, na),
        out_shape=(jax.ShapeDtypeStruct((fb, db), BF16), jax.ShapeDtypeStruct((8, 128), F32)),
        in_specs=[anywhere] * 6 + [pl.BlockSpec(memory_space=pltpu.SMEM)],
        out_specs=[pl.BlockSpec(memory_space=pltpu.VMEM)] * 2,
        scratch_shapes=[
            vmem((fb, db), BF16),
            vmem((nz, part, db), BF16),
            vmem((ra, db), BF16),
            vmem((nz, ra, db), BF16),
            vmem((2, d_all, db), BF16),
            vmem((fb, f_all), BF16),
            vmem((f_all, fb), BF16),
            vmem((fb, db), F32),
            vmem((fb, db), F32),
            vmem((fb, db), F32),
            vmem((fb, archive), BF16),
            vmem((2, part, db), F32),
            vmem((2, part, db), BF16),
            vmem((f_all, db), BF16),
            vmem((archive, db), BF16),
            vmem((f_all, db), BF16),
            vmem((nt, 2, part, db), BF16),
            vmem((2, part, db), BF16),
            vmem((na, fb, db), BF16),
            vmem((2, 2, part, db), BF16),
            vmem((2, 2, reach, part, db), BF16),
            vmem((2, 2, part, db), BF16),
            vmem((part, db), F32),
            vmem((2, part, db), BF16),
            vmem((8, archive), F32),
            vmem((nt, 8, 128), F32),
            vmem((nz, 8, 128), F32),
            dma((6,)), dma((2, 2, 2)), dma((nz, 2)), dma((nz, 2)), one, one,
            dma((nz,)), dma((nz,)),
            one, one, dma((nt,)), dma((nt,)), dma((nt,)), dma((nt,)),
            one, one, dma((nt, 2)), dma((nt, 2)), dma((nt,)), dma((nt,)), dma((nt, 2)), dma((nt, 2)),
            one, one, dma((na, 2)), dma((na, 2)),
            dma((2, 2, 2)), dma((2, 2, reach, 2)), dma((2, 2, reach, 2)), dma((2, 2, 2)), one, one,
            dma((nt,)), dma((nt,)), dma((nz,)), dma((nz,)),
        ],
        compiler_params=pltpu.CompilerParams(
            collective_id=0, has_side_effects=True, vmem_limit_bytes=60 * 2**20
        ),
    )(query_grads, input_basis, output_basis.T, eigenvalues, activations, gradients.T, seq_lengths)
    return pre.T[None], scores[:na, : seq_lengths.shape[1]]


def solution(mesh):
    nz, nt, na = mesh.shape["grp"], mesh.shape["tile"], mesh.shape["arch"]
    return jax.shard_map(
        functools.partial(per_device, nz, nt, na),
        mesh=mesh,
        in_specs=(
            P("arch", "tile", "grp"),
            P(None, "grp"),
            P(None, "tile"),
            P("tile", "grp"),
            P("arch", "grp"),
            P("arch", "tile"),
            P("arch", None),
        ),
        out_specs=(P("arch", "grp", "tile"), P(None, "arch")),
        check_vma=False,
    )
```

```python
import functools

import jax
import jax.numpy as jnp
from jax import lax
from jax.experimental import pallas as pl
from jax.experimental.pallas import tpu as pltpu
from jax.sharding import PartitionSpec as P

damping = 0.01
MESH = pl.DeviceIdType.MESH
BF16, F32 = jnp.bfloat16, jnp.float32


def dot(a, b):
    return jnp.dot(a, b, preferred_element_type=F32)


def dot_last(a, b):
    return lax.dot_general(a, b, (((1,), (1,)), ((), ())), preferred_element_type=F32)


def kernel(
    nz, nt, na,
    q_hbm, u_hbm, vt_hbm, eig_hbm, act_hbm, gt_hbm, len_ref,
    pre_ref, score_ref,
    piece, pieces, act, acts, u, vt, v, eig, eig_pair, inv, gt,
    acc, ybuf, rin, aprime, outgoing, arrived, restored, rall,
    first, chain, final, own, own_pair, tokens, seq_tile, seq_z,
    local_sem, f_send, g_send, g_recv, x_send, x_recv,
    ar_send, ar_recv,
    uz_send, uz_recv, ut_send, ut_recv, uc_send, uc_recv,
    e_send, e_recv, t_send, t_recv, a_send, a_recv, s_send, s_recv,
    p_send, p_recv, q_send, q_recv,
    r0_send, r_send, r_recv, rf_recv, o_send, o_recv,
    pt_send, pt_recv, pz_send, pz_recv,
):
    z, t, a = lax.axis_index("grp"), lax.axis_index("tile"), lax.axis_index("arch")
    fb, db = q_hbm.shape[1], q_hbm.shape[2]
    part = fb // 2
    nc = 2
    half = part // nc
    ra = act_hbm.shape[0] // nt
    d_all = u_hbm.shape[0]
    up = d_all // (2 * nt)
    reach = nz // 4
    core, pair = lax.rem(a, 2), a - lax.rem(a, 2)
    odd = lax.rem(z, 2)
    mine = pair + odd
    same = lax.rem(z + core, 2) == 0
    other_core = a + 1 - 2 * core
    z_pair = z + 1 - 2 * odd
    chunks = tuple(pl.ds(c * half, half) for c in range(nc))

    def at_z(d):
        return lax.rem(z + (d + nz), nz)

    def at_tile(j):
        return lax.rem(t + j, nt)

    def remote(src, dst, send, recv, **dev):
        return pltpu.make_async_remote_copy(
            src_ref=src, dst_ref=dst, send_sem=send, recv_sem=recv, device_id=dev, device_id_type=MESH
        )

    sent = []
    far_first = sorted(range(1, nt), key=lambda j: -(2 * (j >= nt // 2) + min(j % (nt // 2), nt // 2 - j % (nt // 2))))

    def go(copy):
        copy.start()
        sent.append(copy)

    loads = [
        pltpu.make_async_copy(q_hbm.at[0], piece, local_sem.at[0]),
        pltpu.make_async_copy(act_hbm.at[pl.ds(pl.multiple_of(t * ra, ra), ra)], act, local_sem.at[1]),
        pltpu.make_async_copy(u_hbm, u.at[odd], local_sem.at[2]),
        pltpu.make_async_copy(vt_hbm, vt, local_sem.at[3]),
        pltpu.make_async_copy(eig_hbm, eig, local_sem.at[4]),
        pltpu.make_async_copy(gt_hbm, gt, local_sem.at[5]),
    ]
    for load in loads:
        load.start()

    barrier = pltpu.get_barrier_semaphore()
    peers = [{"grp": at_z(d), "arch": pair + h} for d in (1, -1) for h in (0, 1)]
    peers += [{"grp": at_z(d), "arch": pair + h} for d in (2, -2) for h in (0, 1)]
    peers += [{"tile": at_tile(j), "arch": pair + h} for j in range(1, nt) for h in (0, 1)]
    peers += [{"arch": lax.rem(a + j, na)} for j in range(1, na)]
    for peer in peers:
        pl.semaphore_signal(barrier, inc=1, device_id=peer, device_id_type=MESH)
    loads[0].wait()
    pl.semaphore_wait(barrier, len(peers))

    def uz():
        rows = pl.ds(pl.multiple_of((2 * t + core) * up, 128), up)
        return remote(u.at[odd, rows], u.at[odd, rows], uz_send, uz_recv, grp=z_pair)

    def foreign(tile, h):
        return u.at[1 - odd, pl.ds(pl.multiple_of((2 * tile + h) * up, 128), up)]

    def ut(j):
        return remote(foreign(t, core), foreign(t, core), ut_send.at[j], ut_recv.at[j], tile=at_tile(j))

    def uc(j):
        rows = foreign(at_tile(nt - j), core)
        return remote(rows, rows, uc_send.at[j], uc_recv.at[j], arch=other_core)

    hop = 2 - lax.rem(z + core, 2)
    for c in range(nc):
        for h in range(2):
            src = piece.at[pl.ds(h * part + c * half, half)]
            for side, (to, slot) in enumerate(((lax.rem(z + hop, nz), nz - hop), (lax.rem(z + nz - hop, nz), hop))):
                go(remote(
                    src, pieces.at[slot, chunks[c]], f_send.at[side, h, c], g_recv.at[slot, c], grp=to, arch=pair + h
                ))

    def from_core():
        rows = pl.ds(pl.multiple_of((1 - core) * part, 16), part)
        return remote(piece.at[rows], pieces.at[0], x_send, x_recv, arch=other_core)

    @pl.when(same)
    def _():
        from_core().start()
        pieces[0] = piece[pl.ds(pl.multiple_of(core * part, 16), part), :]

    loads[2].wait()
    go(uz())
    for load in (loads[1], *loads[3:]):
        load.wait()

    def urows(d):
        return pl.ds(pl.multiple_of(at_z(d) * db, 128), db)

    own_rows = pl.ds(pl.multiple_of(t * ra, ra), ra)

    def act_product():
        total = dot(act[...], u[odd, urows(0), :])
        for d in range(1, nz):
            remote(act, acts.at[d], ar_send.at[d], ar_recv.at[d], grp=at_z(d)).wait_recv()
            total += dot(acts[d], u[odd, urows(-d), :])
        aprime[own_rows, :] = total.astype(BF16)
        for j in range(1, nt):
            go(remote(aprime.at[own_rows], aprime.at[own_rows], a_send.at[j], a_recv.at[j], tile=at_tile(j)))

    def arrive(slot, c):
        remote(piece.at[chunks[c]], pieces.at[slot, chunks[c]], g_send.at[slot, c], g_recv.at[slot, c], grp=z).wait_recv()

    def forward(slot, c, d):
        to = (slot - d) % nz
        go(remote(
            pieces.at[slot, chunks[c]], pieces.at[to, chunks[c]], g_send.at[to, c], g_recv.at[to, c], grp=at_z(d)
        ))

    v[...] = vt[...].T

    @pl.when(jnp.logical_not(same))
    def _():
        from_core().wait_recv()

    acc[odd] = dot(pieces[0], u[odd, urows(0), :])
    ready = [0]
    for step in range(reach):
        new = []
        if step == reach - 1:
            for j in range(nt):
                if j:
                    ut_from = foreign(at_tile(nt - j), core)
                    remote(ut_from, ut_from, ut_send.at[j], ut_recv.at[j], tile=at_tile(j)).wait_recv()
                go(uc(j))

            @pl.when(same)
            def _():
                remote(eig, eig_pair, e_send, e_recv, grp=z_pair).start()

        for c in range(nc):
            for far in (0, 1):
                for side, d in enumerate((2, -2)):
                    last = reach if far else reach - (c % 2 != side)
                    if step >= last:
                        continue
                    dist = 2 * step + (1 if far else 2)
                    slot = (-dist if side == 0 else dist) % nz
                    arrive(slot, c)
                    if step + 1 < last:
                        forward(slot, c, d)
                    if slot not in new:
                        new.append(slot)
        if step == reach - 1:
            for j in range(nt):
                rows = foreign(at_tile(nt - j), 1 - core)
                remote(rows, rows, uc_send.at[j], uc_recv.at[j], arch=other_core).wait_recv()
        else:
            if step == 0:
                uz_rows = foreign(t, core)
                remote(uz_rows, uz_rows, uz_send, uz_recv, grp=z_pair).wait_recv()
                for j in range(1, nt):
                    go(ut(j))
        for slot in new:
            acc[odd] += dot(pieces[slot], u[odd, urows(slot), :])
        ready += new
    total = dot(pieces[0], u[1 - odd, urows(0), :])
    for slot in ready[1:]:
        total += dot(pieces[slot], u[1 - odd, urows(slot), :])
    ybuf[1 - odd] = total.astype(BF16)
    ybuf[odd] = acc[odd].astype(BF16)

    def rin_rows(tile, h):
        return pl.ds(pl.multiple_of(tile * fb + h * part, 16), part)

    def tile_gather(j, e):
        rows = rin.at[rin_rows(t, core)]
        return remote(
            ybuf.at[e], rows, t_send.at[j, e], t_recv.at[j, core], tile=at_tile(j), arch=pair + e
        )

    for j in far_first:
        for e in range(2):
            go(tile_gather(j, e))
    cross = remote(
        ybuf.at[1 - core], rin.at[rin_rows(t, core)], t_send.at[0, 0], t_recv.at[0, core], arch=other_core
    )
    go(cross)
    rin[rin_rows(t, core), :] = ybuf[core]
    for d in sorted(range(1, nz), key=lambda k: -min(k, nz - k)):
        go(remote(act, acts.at[d], ar_send.at[d], ar_recv.at[d], grp=at_z(d)))

    @pl.when(jnp.logical_not(same))
    def _():
        remote(eig, eig_pair, e_send, e_recv, grp=z_pair).wait_recv()
        inv[...] = 1.0 / (eig_pair[...] + damping)

    @pl.when(same)
    def _():
        inv[...] = 1.0 / (eig[...] + damping)

    def tile_wait(j, h):
        rows = rin.at[rin_rows(at_tile(nt - j), h)]
        remote(rows, rows, t_send.at[j, 0], t_recv.at[j, h], arch=other_core).wait_recv()

    tile_wait(0, 1 - core)
    for j in range(1, nt):
        for h in range(2):
            tile_wait(j, h)
    scaled = (dot(vt[...], rin[...]) * inv[...]).astype(BF16)

    def tile_scatter(j, h):
        src = outgoing.at[rin_rows(at_tile(j), h)]
        return remote(src, arrived.at[j, core], s_send.at[j, h], s_recv.at[j, core], tile=at_tile(j), arch=pair + h)

    def block(j):
        rows = pl.ds(pl.multiple_of(at_tile(j) * fb, 16), fb)
        outgoing[rows, :] = dot(v[rows, :], scaled).astype(BF16)

    for j in far_first:
        block(j)
        for h in range(2):
            go(tile_scatter(j, h))
    block(0)
    go(remote(
        outgoing.at[rin_rows(t, 1 - core)], arrived.at[0, core], s_send.at[0, 0], s_recv.at[0, core], arch=other_core
    ))
    arrived[0, core] = outgoing[rin_rows(t, core), :]

    def scatter_wait(j, e):
        dst = arrived.at[j, e]
        remote(dst, dst, s_send.at[j, 0], s_recv.at[j, e], arch=other_core).wait_recv()

    scatter_wait(0, 1 - core)
    for j in range(1, nt):
        for e in range(2):
            scatter_wait(j, e)
    for e in range(2):
        total = arrived[0, e].astype(F32)
        for j in range(1, nt):
            total += arrived[j, e].astype(F32)
        restored[e] = total.astype(BF16)

    def share(d):
        rows = urows(d)
        return dot_last(restored[0], u[0, rows, :]) + dot_last(restored[1], u[1, rows, :])

    def lasts(far, side):
        return tuple(reach if far else reach - (c % 2 != side) for c in range(nc))

    def scatter(step, c, far, side):
        last = lasts(far, side)[c]
        src = first.at[far, side, chunks[c]] if step == 0 else chain.at[far, side, step - 1, chunks[c]]
        d = 2 if side == 0 else -2
        if step < last - 1:
            return remote(
                src, chain.at[far, side, step, chunks[c]], r_send.at[far, side, step, c],
                r_recv.at[far, side, step, c], grp=at_z(d),
            )
        return remote(
            src, final.at[side, core, chunks[c]], r0_send.at[far, side, c], rf_recv.at[side, core, c],
            grp=at_z(d // 2 if far else d), arch=mine,
        )

    def distance(step, c, far, side):
        m = 2 * (lasts(far, side)[c] - step) - far
        return m if side == 0 else -m

    core_rows = pl.ds(pl.multiple_of(core * part, 16), part)
    rall[mine, core_rows, :] = restored[odd]
    go(remote(restored.at[1 - odd], rall.at[mine, core_rows], p_send, p_recv, grp=z_pair))
    for j in range(1, na):
        go(remote(
            rall.at[mine, core_rows], rall.at[mine, core_rows], q_send.at[j, 0], q_recv.at[j, 0], arch=lax.rem(a + j, na)
        ))

    for far in (0, 1):
        for side in range(2):
            terms = {}
            for c in range(nc):
                m = distance(0, c, far, side)
                if m not in terms:
                    terms[m] = share(m)
                first[far, side, chunks[c], :] = terms[m][c * half:(c + 1) * half].astype(BF16)
                go(scatter(0, c, far, side))

    act_product()

    def spread():
        slot = rall.at[pair + 1 - odd, core_rows]
        remote(slot, slot, p_send, p_recv, grp=z_pair).wait_recv()
        for j in range(1, na):
            go(remote(slot, slot, q_send.at[j, 1], q_recv.at[j, 1], arch=lax.rem(a + j, na)))

    def token(q):
        product = dot_last(rall[q], aprime[...]) * gt[...].astype(F32)
        tokens[pl.ds(q, 1), :] = jnp.sum(product, axis=0, keepdims=True)

    def arch_wait(which):
        for j in range(1, na):
            src = lax.rem(a + (na - j), na)
            src_core = lax.rem(src, 2)
            q = src - src_core + (odd if which == 0 else 1 - odd)
            slot = rall.at[q, pl.ds(pl.multiple_of(src_core * part, 16), part)]
            remote(slot, slot, q_send.at[j, which], q_recv.at[j, which], arch=src).wait_recv()

    def scores():
        position = lax.broadcasted_iota(jnp.int32, (8, nt * ra), 1)
        lane = lax.broadcasted_iota(jnp.int32, (8, 128), 1)
        line = jnp.zeros((8, 128), F32)
        start = jnp.int32(0)
        for s in range(len_ref.shape[1]):
            end = start + len_ref[0, s]
            inside = jnp.logical_and(position >= start, position < end)
            one = jnp.sum(jnp.where(inside, tokens[...], 0.0), axis=1, keepdims=True)
            line = jnp.where(lane == s, one, line)
            start = end
        seq_tile[t] = line
        for j in range(1, nt):
            go(remote(seq_tile.at[t], seq_tile.at[t], pt_send.at[j], pt_recv.at[j], tile=at_tile(j)))

    def sum_tile():
        for j in range(1, nt):
            slot = seq_tile.at[at_tile(nt - j)]
            remote(slot, slot, pt_send.at[j], pt_recv.at[j], tile=at_tile(j)).wait_recv()
        total = seq_tile[0]
        for i in range(1, nt):
            total += seq_tile[i]
        seq_z[z] = total
        for d in range(1, nz):
            go(remote(seq_z.at[z], seq_z.at[z], pz_send.at[d], pz_recv.at[d], grp=at_z(d)))

    def sum_z():
        for d in range(1, nz):
            slot = seq_z.at[at_z(-d)]
            remote(slot, slot, pz_send.at[d], pz_recv.at[d], grp=at_z(d)).wait_recv()
        total = seq_z[0]
        for i in range(1, nz):
            total += seq_z[i]
        lane = lax.broadcasted_iota(jnp.int32, (1, 128), 1)
        sizes = jnp.ones((1, 128), F32)
        for s in range(len_ref.shape[1]):
            sizes = jnp.where(lane == s, len_ref[0, s].astype(F32), sizes)
        score_ref[...] = (total / sizes)[:na, : len_ref.shape[1]]

    spread()
    for step in range(1, reach):
        for far in (0, 1):
            for side in range(2):
                terms = {}
                for c in range(nc):
                    if step < lasts(far, side)[c]:
                        m = distance(step, c, far, side)
                        if m not in terms:
                            terms[m] = share(m)
                for c in range(nc):
                    if step >= lasts(far, side)[c]:
                        continue
                    m = distance(step, c, far, side)
                    scatter(step - 1, c, far, side).wait_recv()
                    got = chain[far, side, step - 1, chunks[c], :].astype(F32)
                    chain[far, side, step - 1, chunks[c], :] = (
                        got + terms[m][c * half:(c + 1) * half]
                    ).astype(BF16)
                    go(scatter(step, c, far, side))
        if step == 1:
            own[...] = share(0)

            @pl.when(jnp.logical_not(same))
            def _():
                own_pair[0] = own[...].astype(BF16)
                remote(own_pair.at[0], own_pair.at[1], o_send, o_recv, arch=other_core).start()

            tokens[...] = jnp.zeros_like(tokens)
            for j in range(1, nt):
                place = aprime.at[pl.ds(pl.multiple_of(at_tile(nt - j) * ra, ra), ra)]
                remote(place, place, a_send.at[j], a_recv.at[j], tile=at_tile(j)).wait_recv()
            for which in range(2):
                arch_wait(which)
                q = odd if which == 0 else 1 - odd
                token(q)
                token(2 + q)
            scores()
        if step == max(reach - 2, 2):
            sum_tile()

    if reach == 2:
        sum_tile()
    for side in range(2):
        for h in range(2):
            for c in range(nc):
                slot = final.at[side, h, chunks[c]]
                remote(slot, slot, r0_send.at[0, side, c], rf_recv.at[side, h, c], grp=z_pair).wait_recv()
    for h in range(2):
        total = final[0, h].astype(F32) + final[1, h].astype(F32)
        pre_ref[pl.ds(h * part, part), :] = total.astype(BF16)

    @pl.when(same)
    def _():
        remote(own_pair.at[0], own_pair.at[1], o_send, o_recv, arch=other_core).wait_recv()
        for h, term in ((core, own[...]), (1 - core, own_pair[1].astype(F32))):
            total = final[0, h].astype(F32) + final[1, h].astype(F32) + term
            pre_ref[pl.ds(pl.multiple_of(h * part, 16), part), :] = total.astype(BF16)

    sum_z()
    for copy in sent:
        copy.wait_send()

    @pl.when(same)
    def _():
        from_core().wait_send()
        remote(eig, eig_pair, e_send, e_recv, grp=z_pair).wait_send()

    @pl.when(jnp.logical_not(same))
    def _():
        remote(own_pair.at[0], own_pair.at[1], o_send, o_recv, arch=other_core).wait_send()


def per_device(nz, nt, na, query_grads, input_basis, output_basis, eigenvalues, activations, gradients, seq_lengths):
    fb, db = query_grads.shape[1:]
    d_all, f_all = input_basis.shape[0], output_basis.shape[0]
    archive = activations.shape[0]
    ra = archive // nt
    part = fb // 2
    nc = 2
    reach = nz // 4
    anywhere = pl.BlockSpec(memory_space=pl.ANY)
    dma = pltpu.SemaphoreType.DMA
    vmem = pltpu.VMEM
    one = dma(())
    pre, scores = pl.pallas_call(
        functools.partial(kernel, nz, nt, na),
        out_shape=(jax.ShapeDtypeStruct((fb, db), BF16), jax.ShapeDtypeStruct((na, seq_lengths.shape[1]), F32)),
        in_specs=[anywhere] * 6 + [pl.BlockSpec(memory_space=pltpu.SMEM)],
        out_specs=[pl.BlockSpec(memory_space=pltpu.VMEM)] * 2,
        scratch_shapes=[
            vmem((fb, db), BF16),
            vmem((nz, part, db), BF16),
            vmem((ra, db), BF16),
            vmem((nz, ra, db), BF16),
            vmem((2, d_all, db), BF16),
            vmem((fb, f_all), BF16),
            vmem((f_all, fb), BF16),
            vmem((fb, db), F32),
            vmem((fb, db), F32),
            vmem((fb, db), F32),
            vmem((fb, archive), BF16),
            vmem((2, part, db), F32),
            vmem((2, part, db), BF16),
            vmem((f_all, db), BF16),
            vmem((archive, db), BF16),
            vmem((f_all, db), BF16),
            vmem((nt, 2, part, db), BF16),
            vmem((2, part, db), BF16),
            vmem((na, fb, db), BF16),
            vmem((2, 2, part, db), BF16),
            vmem((2, 2, reach, part, db), BF16),
            vmem((2, 2, part, db), BF16),
            vmem((part, db), F32),
            vmem((2, part, db), BF16),
            vmem((8, archive), F32),
            vmem((nt, 8, 128), F32),
            vmem((nz, 8, 128), F32),
            dma((6,)), dma((2, 2, nc)), dma((nz, nc)), dma((nz, nc)), one, one,
            dma((nz,)), dma((nz,)),
            one, one, dma((nt,)), dma((nt,)), dma((nt,)), dma((nt,)),
            one, one, dma((nt, 2)), dma((nt, 2)), dma((nt,)), dma((nt,)), dma((nt, 2)), dma((nt, 2)),
            one, one, dma((na, 2)), dma((na, 2)),
            dma((2, 2, nc)), dma((2, 2, reach, nc)), dma((2, 2, reach, nc)), dma((2, 2, nc)), one, one,
            dma((nt,)), dma((nt,)), dma((nz,)), dma((nz,)),
        ],
        compiler_params=pltpu.CompilerParams(
            collective_id=0, has_side_effects=True, vmem_limit_bytes=60 * 2**20
        ),
    )(query_grads, input_basis, output_basis.T, eigenvalues, activations, gradients.T, seq_lengths)
    return pre.T[None], scores


def solution(mesh):
    nz, nt, na = mesh.shape["grp"], mesh.shape["tile"], mesh.shape["arch"]
    return jax.shard_map(
        functools.partial(per_device, nz, nt, na),
        mesh=mesh,
        in_specs=(
            P("arch", "tile", "grp"),
            P(None, "grp"),
            P(None, "tile"),
            P("tile", "grp"),
            P("arch", "grp"),
            P("arch", "tile"),
            P("arch", None),
        ),
        out_specs=(P("arch", "grp", "tile"), P(None, "arch")),
        check_vma=False,
    )
```

```python
import functools

import jax
import jax.numpy as jnp
from jax import lax
from jax.experimental import pallas as pl
from jax.experimental.pallas import tpu as pltpu
from jax.sharding import PartitionSpec as P

damping = 0.01
MESH = pl.DeviceIdType.MESH
BF16, F32 = jnp.bfloat16, jnp.float32


def dot(a, b):
    return jnp.dot(a, b, preferred_element_type=F32)


def dot_last(a, b):
    return lax.dot_general(a, b, (((1,), (1,)), ((), ())), preferred_element_type=F32)


def kernel(
    nz, nt, na,
    q_hbm, u_hbm, vt_hbm, eig_hbm, act_hbm, gt_hbm, len_ref,
    pre_ref, score_ref,
    piece, pieces, act, acts, u, vt, v, eig, eig_pair, inv, gt,
    acc, ybuf, rin, aprime, outgoing, arrived, restored, rall,
    first, chain, final, own, own_pair, tokens, seq_tile, seq_z,
    local_sem, f_send, g_send, g_recv, x_send, x_recv,
    ar_send, ar_recv,
    uz_send, uz_recv, ut_send, ut_recv, uc_send, uc_recv,
    e_send, e_recv, t_send, t_recv, a_send, a_recv, s_send, s_recv,
    p_send, p_recv, q_send, q_recv,
    r0_send, r_send, r_recv, rf_recv, o_send, o_recv,
    pt_send, pt_recv, pz_send, pz_recv,
):
    z, t, a = lax.axis_index("grp"), lax.axis_index("tile"), lax.axis_index("arch")
    fb, db = q_hbm.shape[1], q_hbm.shape[2]
    part = fb // 2
    nc = 2
    half = part // nc
    ra = act_hbm.shape[0] // nt
    d_all = u_hbm.shape[0]
    up = d_all // (2 * nt)
    reach = nz // 4
    core, pair = lax.rem(a, 2), a - lax.rem(a, 2)
    odd = lax.rem(z, 2)
    mine = pair + odd
    same = lax.rem(z + core, 2) == 0
    other_core = a + 1 - 2 * core
    z_pair = z + 1 - 2 * odd
    chunks = tuple(pl.ds(c * half, half) for c in range(nc))

    def at_z(d):
        return lax.rem(z + (d + nz), nz)

    def at_tile(j):
        return lax.rem(t + j, nt)

    def remote(src, dst, send, recv, **dev):
        return pltpu.make_async_remote_copy(
            src_ref=src, dst_ref=dst, send_sem=send, recv_sem=recv, device_id=dev, device_id_type=MESH
        )

    sent = []
    far_first = sorted(range(1, nt), key=lambda j: -(2 * (j >= nt // 2) + min(j % (nt // 2), nt // 2 - j % (nt // 2))))

    def go(copy):
        copy.start()
        sent.append(copy)

    loads = [
        pltpu.make_async_copy(q_hbm.at[0], piece, local_sem.at[0]),
        pltpu.make_async_copy(act_hbm.at[pl.ds(pl.multiple_of(t * ra, ra), ra)], act, local_sem.at[1]),
        pltpu.make_async_copy(u_hbm, u.at[odd], local_sem.at[2]),
        pltpu.make_async_copy(vt_hbm, vt, local_sem.at[3]),
        pltpu.make_async_copy(eig_hbm, eig, local_sem.at[4]),
        pltpu.make_async_copy(gt_hbm, gt, local_sem.at[5]),
    ]
    for load in loads:
        load.start()

    barrier = pltpu.get_barrier_semaphore()
    peers = [{"grp": at_z(d), "arch": pair + h} for d in (1, -1) for h in (0, 1)]
    peers += [{"grp": at_z(d), "arch": pair + h} for d in (2, -2) for h in (0, 1)]
    peers += [{"tile": at_tile(j), "arch": pair + h} for j in range(1, nt) for h in (0, 1)]
    peers += [{"arch": lax.rem(a + j, na)} for j in range(1, na)]
    for peer in peers:
        pl.semaphore_signal(barrier, inc=1, device_id=peer, device_id_type=MESH)
    loads[0].wait()
    pl.semaphore_wait(barrier, len(peers))

    def uz():
        rows = pl.ds(pl.multiple_of((2 * t + core) * up, 128), up)
        return remote(u.at[odd, rows], u.at[odd, rows], uz_send, uz_recv, grp=z_pair)

    def foreign(tile, h):
        return u.at[1 - odd, pl.ds(pl.multiple_of((2 * tile + h) * up, 128), up)]

    def ut(j):
        return remote(foreign(t, core), foreign(t, core), ut_send.at[j], ut_recv.at[j], tile=at_tile(j))

    def uc(j):
        rows = foreign(at_tile(nt - j), core)
        return remote(rows, rows, uc_send.at[j], uc_recv.at[j], arch=other_core)

    hop = 2 - lax.rem(z + core, 2)
    for c in range(nc):
        for h in range(2):
            src = piece.at[pl.ds(h * part + c * half, half)]
            for side, (to, slot) in enumerate(((lax.rem(z + hop, nz), nz - hop), (lax.rem(z + nz - hop, nz), hop))):
                go(remote(
                    src, pieces.at[slot, chunks[c]], f_send.at[side, h, c], g_recv.at[slot, c], grp=to, arch=pair + h
                ))

    def from_core():
        rows = pl.ds(pl.multiple_of((1 - core) * part, 16), part)
        return remote(piece.at[rows], pieces.at[0], x_send, x_recv, arch=other_core)

    @pl.when(same)
    def _():
        from_core().start()
        pieces[0] = piece[pl.ds(pl.multiple_of(core * part, 16), part), :]

    loads[2].wait()
    go(uz())
    for load in (loads[1], *loads[3:]):
        load.wait()

    def urows(d):
        return pl.ds(pl.multiple_of(at_z(d) * db, 128), db)

    own_rows = pl.ds(pl.multiple_of(t * ra, ra), ra)

    def act_product():
        total = dot(act[...], u[odd, urows(0), :])
        for d in range(1, nz):
            remote(act, acts.at[d], ar_send.at[d], ar_recv.at[d], grp=at_z(d)).wait_recv()
            total += dot(acts[d], u[odd, urows(-d), :])
        aprime[own_rows, :] = total.astype(BF16)
        for j in far_first:
            go(remote(aprime.at[own_rows], aprime.at[own_rows], a_send.at[j], a_recv.at[j], tile=at_tile(j)))

    def arrive(slot, c):
        remote(piece.at[chunks[c]], pieces.at[slot, chunks[c]], g_send.at[slot, c], g_recv.at[slot, c], grp=z).wait_recv()

    def forward(slot, c, d):
        to = (slot - d) % nz
        go(remote(
            pieces.at[slot, chunks[c]], pieces.at[to, chunks[c]], g_send.at[to, c], g_recv.at[to, c], grp=at_z(d)
        ))

    v[...] = vt[...].T

    @pl.when(jnp.logical_not(same))
    def _():
        from_core().wait_recv()

    acc[odd] = dot(pieces[0], u[odd, urows(0), :])
    ready = [0]
    for step in range(reach):
        new = []
        if step == reach - 1:
            for j in range(nt):
                if j:
                    ut_from = foreign(at_tile(nt - j), core)
                    remote(ut_from, ut_from, ut_send.at[j], ut_recv.at[j], tile=at_tile(j)).wait_recv()
                go(uc(j))

            @pl.when(same)
            def _():
                remote(eig, eig_pair, e_send, e_recv, grp=z_pair).start()

        for c in range(nc):
            for far in (0, 1):
                for side, d in enumerate((2, -2)):
                    last = reach if far else reach - (c % 2 != side)
                    if step >= last:
                        continue
                    dist = 2 * step + (1 if far else 2)
                    slot = (-dist if side == 0 else dist) % nz
                    arrive(slot, c)
                    if step + 1 < last:
                        forward(slot, c, d)
                    if slot not in new:
                        new.append(slot)
        if step == reach - 1:
            for j in range(nt):
                rows = foreign(at_tile(nt - j), 1 - core)
                remote(rows, rows, uc_send.at[j], uc_recv.at[j], arch=other_core).wait_recv()
        else:
            if step == 0:
                uz_rows = foreign(t, core)
                remote(uz_rows, uz_rows, uz_send, uz_recv, grp=z_pair).wait_recv()
                for j in far_first:
                    go(ut(j))
        for slot in new:
            acc[odd] += dot(pieces[slot], u[odd, urows(slot), :])
        ready += new
    total = dot(pieces[0], u[1 - odd, urows(0), :])
    for slot in ready[1:]:
        total += dot(pieces[slot], u[1 - odd, urows(slot), :])
    ybuf[1 - odd] = total.astype(BF16)
    ybuf[odd] = acc[odd].astype(BF16)

    def rin_rows(tile, h):
        return pl.ds(pl.multiple_of(tile * fb + h * part, 16), part)

    def tile_gather(j, e):
        rows = rin.at[rin_rows(t, core)]
        return remote(
            ybuf.at[e], rows, t_send.at[j, e], t_recv.at[j, core], tile=at_tile(j), arch=pair + e
        )

    for j in far_first:
        for e in range(2):
            go(tile_gather(j, e))
    cross = remote(
        ybuf.at[1 - core], rin.at[rin_rows(t, core)], t_send.at[0, 0], t_recv.at[0, core], arch=other_core
    )
    go(cross)
    rin[rin_rows(t, core), :] = ybuf[core]
    for d in sorted(range(1, nz), key=lambda k: -min(k, nz - k)):
        go(remote(act, acts.at[d], ar_send.at[d], ar_recv.at[d], grp=at_z(d)))

    @pl.when(jnp.logical_not(same))
    def _():
        remote(eig, eig_pair, e_send, e_recv, grp=z_pair).wait_recv()
        inv[...] = 1.0 / (eig_pair[...] + damping)

    @pl.when(same)
    def _():
        inv[...] = 1.0 / (eig[...] + damping)

    def tile_wait(j, h):
        rows = rin.at[rin_rows(at_tile(nt - j), h)]
        remote(rows, rows, t_send.at[j, 0], t_recv.at[j, h], arch=other_core).wait_recv()

    tile_wait(0, 1 - core)
    for j in range(1, nt):
        for h in range(2):
            tile_wait(j, h)
    scaled = (dot(vt[...], rin[...]) * inv[...]).astype(BF16)

    def tile_scatter(j, h):
        src = outgoing.at[rin_rows(at_tile(j), h)]
        return remote(src, arrived.at[j, core], s_send.at[j, h], s_recv.at[j, core], tile=at_tile(j), arch=pair + h)

    def block(j):
        rows = pl.ds(pl.multiple_of(at_tile(j) * fb, 16), fb)
        outgoing[rows, :] = dot(v[rows, :], scaled).astype(BF16)

    for j in far_first:
        block(j)
        for h in range(2):
            go(tile_scatter(j, h))
    block(0)
    go(remote(
        outgoing.at[rin_rows(t, 1 - core)], arrived.at[0, core], s_send.at[0, 0], s_recv.at[0, core], arch=other_core
    ))
    arrived[0, core] = outgoing[rin_rows(t, core), :]

    def scatter_wait(j, e):
        dst = arrived.at[j, e]
        remote(dst, dst, s_send.at[j, 0], s_recv.at[j, e], arch=other_core).wait_recv()

    scatter_wait(0, 1 - core)
    for j in range(1, nt):
        for e in range(2):
            scatter_wait(j, e)
    for e in range(2):
        total = arrived[0, e].astype(F32)
        for j in range(1, nt):
            total += arrived[j, e].astype(F32)
        restored[e] = total.astype(BF16)

    def share(d):
        rows = urows(d)
        return dot_last(restored[0], u[0, rows, :]) + dot_last(restored[1], u[1, rows, :])

    def lasts(far, side):
        return tuple(reach if far else reach - (c % 2 != side) for c in range(nc))

    def scatter(step, c, far, side):
        last = lasts(far, side)[c]
        src = first.at[far, side, chunks[c]] if step == 0 else chain.at[far, side, step - 1, chunks[c]]
        d = 2 if side == 0 else -2
        if step < last - 1:
            return remote(
                src, chain.at[far, side, step, chunks[c]], r_send.at[far, side, step, c],
                r_recv.at[far, side, step, c], grp=at_z(d),
            )
        return remote(
            src, final.at[side, core, chunks[c]], r0_send.at[far, side, c], rf_recv.at[side, core, c],
            grp=at_z(d // 2 if far else d), arch=mine,
        )

    def distance(step, c, far, side):
        m = 2 * (lasts(far, side)[c] - step) - far
        return m if side == 0 else -m

    core_rows = pl.ds(pl.multiple_of(core * part, 16), part)
    rall[mine, core_rows, :] = restored[odd]
    go(remote(restored.at[1 - odd], rall.at[mine, core_rows], p_send, p_recv, grp=z_pair))
    for j in range(1, na):
        go(remote(
            rall.at[mine, core_rows], rall.at[mine, core_rows], q_send.at[j, 0], q_recv.at[j, 0], arch=lax.rem(a + j, na)
        ))

    for far in (0, 1):
        for side in range(2):
            terms = {}
            for c in range(nc):
                m = distance(0, c, far, side)
                if m not in terms:
                    terms[m] = share(m)
                first[far, side, chunks[c], :] = terms[m][c * half:(c + 1) * half].astype(BF16)
                go(scatter(0, c, far, side))

    act_product()

    def spread():
        slot = rall.at[pair + 1 - odd, core_rows]
        remote(slot, slot, p_send, p_recv, grp=z_pair).wait_recv()
        for j in range(1, na):
            go(remote(slot, slot, q_send.at[j, 1], q_recv.at[j, 1], arch=lax.rem(a + j, na)))

    def token(q):
        product = dot_last(rall[q], aprime[...]) * gt[...].astype(F32)
        tokens[pl.ds(q, 1), :] = jnp.sum(product, axis=0, keepdims=True)

    def arch_wait(which):
        for j in range(1, na):
            src = lax.rem(a + (na - j), na)
            src_core = lax.rem(src, 2)
            q = src - src_core + (odd if which == 0 else 1 - odd)
            slot = rall.at[q, pl.ds(pl.multiple_of(src_core * part, 16), part)]
            remote(slot, slot, q_send.at[j, which], q_recv.at[j, which], arch=src).wait_recv()

    def scores():
        position = lax.broadcasted_iota(jnp.int32, (8, nt * ra), 1)
        lane = lax.broadcasted_iota(jnp.int32, (8, 128), 1)
        line = jnp.zeros((8, 128), F32)
        start = jnp.int32(0)
        for s in range(len_ref.shape[1]):
            end = start + len_ref[0, s]
            inside = jnp.logical_and(position >= start, position < end)
            one = jnp.sum(jnp.where(inside, tokens[...], 0.0), axis=1, keepdims=True)
            line = jnp.where(lane == s, one, line)
            start = end
        seq_tile[t] = line
        for j in far_first:
            go(remote(seq_tile.at[t], seq_tile.at[t], pt_send.at[j], pt_recv.at[j], tile=at_tile(j)))

    def sum_tile():
        for j in range(1, nt):
            slot = seq_tile.at[at_tile(nt - j)]
            remote(slot, slot, pt_send.at[j], pt_recv.at[j], tile=at_tile(j)).wait_recv()
        total = seq_tile[0]
        for i in range(1, nt):
            total += seq_tile[i]
        seq_z[z] = total
        for d in sorted(range(1, nz), key=lambda k: -min(k, nz - k)):
            go(remote(seq_z.at[z], seq_z.at[z], pz_send.at[d], pz_recv.at[d], grp=at_z(d)))

    def sum_z():
        for d in range(1, nz):
            slot = seq_z.at[at_z(-d)]
            remote(slot, slot, pz_send.at[d], pz_recv.at[d], grp=at_z(d)).wait_recv()
        total = seq_z[0]
        for i in range(1, nz):
            total += seq_z[i]
        lane = lax.broadcasted_iota(jnp.int32, (1, 128), 1)
        sizes = jnp.ones((1, 128), F32)
        for s in range(len_ref.shape[1]):
            sizes = jnp.where(lane == s, len_ref[0, s].astype(F32), sizes)
        score_ref[...] = (total / sizes)[:na, : len_ref.shape[1]]

    spread()
    for step in range(1, reach):
        for far in (0, 1):
            for side in range(2):
                terms = {}
                for c in range(nc):
                    if step < lasts(far, side)[c]:
                        m = distance(step, c, far, side)
                        if m not in terms:
                            terms[m] = share(m)
                for c in range(nc):
                    if step >= lasts(far, side)[c]:
                        continue
                    m = distance(step, c, far, side)
                    scatter(step - 1, c, far, side).wait_recv()
                    got = chain[far, side, step - 1, chunks[c], :].astype(F32)
                    chain[far, side, step - 1, chunks[c], :] = (
                        got + terms[m][c * half:(c + 1) * half]
                    ).astype(BF16)
                    go(scatter(step, c, far, side))
        if step == 1:
            own[...] = share(0)

            @pl.when(jnp.logical_not(same))
            def _():
                own_pair[0] = own[...].astype(BF16)
                remote(own_pair.at[0], own_pair.at[1], o_send, o_recv, arch=other_core).start()

            tokens[...] = jnp.zeros_like(tokens)
            for j in range(1, nt):
                place = aprime.at[pl.ds(pl.multiple_of(at_tile(nt - j) * ra, ra), ra)]
                remote(place, place, a_send.at[j], a_recv.at[j], tile=at_tile(j)).wait_recv()
            for which in range(2):
                arch_wait(which)
                q = odd if which == 0 else 1 - odd
                token(q)
                token(2 + q)
            scores()
        if step == max(reach - 2, 2):
            sum_tile()

    if reach == 2:
        sum_tile()
    for side in range(2):
        for h in range(2):
            for c in range(nc):
                slot = final.at[side, h, chunks[c]]
                remote(slot, slot, r0_send.at[0, side, c], rf_recv.at[side, h, c], grp=z_pair).wait_recv()
    for h in range(2):
        total = final[0, h].astype(F32) + final[1, h].astype(F32)
        pre_ref[pl.ds(h * part, part), :] = total.astype(BF16)

    @pl.when(same)
    def _():
        remote(own_pair.at[0], own_pair.at[1], o_send, o_recv, arch=other_core).wait_recv()
        for h, term in ((core, own[...]), (1 - core, own_pair[1].astype(F32))):
            total = final[0, h].astype(F32) + final[1, h].astype(F32) + term
            pre_ref[pl.ds(pl.multiple_of(h * part, 16), part), :] = total.astype(BF16)

    sum_z()
    for copy in sent:
        copy.wait_send()

    @pl.when(same)
    def _():
        from_core().wait_send()
        remote(eig, eig_pair, e_send, e_recv, grp=z_pair).wait_send()

    @pl.when(jnp.logical_not(same))
    def _():
        remote(own_pair.at[0], own_pair.at[1], o_send, o_recv, arch=other_core).wait_send()


def per_device(nz, nt, na, query_grads, input_basis, output_basis, eigenvalues, activations, gradients, seq_lengths):
    fb, db = query_grads.shape[1:]
    d_all, f_all = input_basis.shape[0], output_basis.shape[0]
    archive = activations.shape[0]
    ra = archive // nt
    part = fb // 2
    nc = 2
    reach = nz // 4
    anywhere = pl.BlockSpec(memory_space=pl.ANY)
    dma = pltpu.SemaphoreType.DMA
    vmem = pltpu.VMEM
    one = dma(())
    pre, scores = pl.pallas_call(
        functools.partial(kernel, nz, nt, na),
        out_shape=(jax.ShapeDtypeStruct((fb, db), BF16), jax.ShapeDtypeStruct((na, seq_lengths.shape[1]), F32)),
        in_specs=[anywhere] * 6 + [pl.BlockSpec(memory_space=pltpu.SMEM)],
        out_specs=[pl.BlockSpec(memory_space=pltpu.VMEM)] * 2,
        scratch_shapes=[
            vmem((fb, db), BF16),
            vmem((nz, part, db), BF16),
            vmem((ra, db), BF16),
            vmem((nz, ra, db), BF16),
            vmem((2, d_all, db), BF16),
            vmem((fb, f_all), BF16),
            vmem((f_all, fb), BF16),
            vmem((fb, db), F32),
            vmem((fb, db), F32),
            vmem((fb, db), F32),
            vmem((fb, archive), BF16),
            vmem((2, part, db), F32),
            vmem((2, part, db), BF16),
            vmem((f_all, db), BF16),
            vmem((archive, db), BF16),
            vmem((f_all, db), BF16),
            vmem((nt, 2, part, db), BF16),
            vmem((2, part, db), BF16),
            vmem((na, fb, db), BF16),
            vmem((2, 2, part, db), BF16),
            vmem((2, 2, reach, part, db), BF16),
            vmem((2, 2, part, db), BF16),
            vmem((part, db), F32),
            vmem((2, part, db), BF16),
            vmem((8, archive), F32),
            vmem((nt, 8, 128), F32),
            vmem((nz, 8, 128), F32),
            dma((6,)), dma((2, 2, nc)), dma((nz, nc)), dma((nz, nc)), one, one,
            dma((nz,)), dma((nz,)),
            one, one, dma((nt,)), dma((nt,)), dma((nt,)), dma((nt,)),
            one, one, dma((nt, 2)), dma((nt, 2)), dma((nt,)), dma((nt,)), dma((nt, 2)), dma((nt, 2)),
            one, one, dma((na, 2)), dma((na, 2)),
            dma((2, 2, nc)), dma((2, 2, reach, nc)), dma((2, 2, reach, nc)), dma((2, 2, nc)), one, one,
            dma((nt,)), dma((nt,)), dma((nz,)), dma((nz,)),
        ],
        compiler_params=pltpu.CompilerParams(
            collective_id=0, has_side_effects=True, vmem_limit_bytes=54 * 2**20
        ),
    )(query_grads, input_basis, output_basis.T, eigenvalues, activations, gradients.T, seq_lengths)
    return pre.T[None], scores


def solution(mesh):
    nz, nt, na = mesh.shape["grp"], mesh.shape["tile"], mesh.shape["arch"]
    return jax.shard_map(
        functools.partial(per_device, nz, nt, na),
        mesh=mesh,
        in_specs=(
            P("arch", "tile", "grp"),
            P(None, "grp"),
            P(None, "tile"),
            P("tile", "grp"),
            P("arch", "grp"),
            P("arch", "tile"),
            P("arch", None),
        ),
        out_specs=(P("arch", "grp", "tile"), P(None, "arch")),
        check_vma=False,
    )
```

```python
import functools

import jax
import jax.numpy as jnp
from jax import lax
from jax.experimental import pallas as pl
from jax.experimental.pallas import tpu as pltpu
from jax.sharding import PartitionSpec as P

damping = 0.01
MESH = pl.DeviceIdType.MESH
BF16, F32 = jnp.bfloat16, jnp.float32


def dot(a, b):
    return jnp.dot(a, b, preferred_element_type=F32)


def dot_last(a, b):
    return lax.dot_general(a, b, (((1,), (1,)), ((), ())), preferred_element_type=F32)


def kernel(
    nz, nt, na,
    q_hbm, u_hbm, vt_hbm, eig_hbm, act_hbm, gt_hbm, len_ref,
    pre_ref, score_ref,
    piece, pieces, act, acts, u, vt, v, eig, eig_pair, inv, gt,
    acc, ybuf, rin, aprime, outgoing, arrived, restored, rall,
    first, chain, final, own, own_pair, tokens, seq_tile, seq_z,
    local_sem, f_send, g_send, g_recv, x_send, x_recv,
    ar_send, ar_recv,
    uz_send, uz_recv, ut_send, ut_recv, uc_send, uc_recv,
    e_send, e_recv, t_send, t_recv, a_send, a_recv, s_send, s_recv,
    p_send, p_recv, q_send, q_recv,
    r0_send, r_send, r_recv, rf_recv, o_send, o_recv,
    pt_send, pt_recv, pz_send, pz_recv,
):
    z, t, a = lax.axis_index("grp"), lax.axis_index("tile"), lax.axis_index("arch")
    fb, db = q_hbm.shape[1], q_hbm.shape[2]
    part = fb // 2
    nc = 2
    half = part // nc
    ra = act_hbm.shape[0] // nt
    d_all = u_hbm.shape[0]
    up = d_all // (2 * nt)
    reach = nz // 4
    core, pair = lax.rem(a, 2), a - lax.rem(a, 2)
    odd = lax.rem(z, 2)
    mine = pair + odd
    same = lax.rem(z + core, 2) == 0
    other_core = a + 1 - 2 * core
    z_pair = z + 1 - 2 * odd
    chunks = tuple(pl.ds(c * half, half) for c in range(nc))

    def at_z(d):
        return lax.rem(z + (d + nz), nz)

    def at_tile(j):
        return lax.rem(t + j, nt)

    def remote(src, dst, send, recv, **dev):
        return pltpu.make_async_remote_copy(
            src_ref=src, dst_ref=dst, send_sem=send, recv_sem=recv, device_id=dev, device_id_type=MESH
        )

    sent = []
    far_first = sorted(range(1, nt), key=lambda j: -(2 * (j >= nt // 2) + min(j % (nt // 2), nt // 2 - j % (nt // 2))))

    def go(copy):
        copy.start()
        sent.append(copy)

    loads = [
        pltpu.make_async_copy(q_hbm.at[0], piece, local_sem.at[0]),
        pltpu.make_async_copy(act_hbm.at[pl.ds(pl.multiple_of(t * ra, ra), ra)], act, local_sem.at[1]),
        pltpu.make_async_copy(u_hbm, u.at[odd], local_sem.at[2]),
        pltpu.make_async_copy(vt_hbm, vt, local_sem.at[3]),
        pltpu.make_async_copy(eig_hbm, eig, local_sem.at[4]),
        pltpu.make_async_copy(gt_hbm, gt, local_sem.at[5]),
    ]
    for load in loads:
        load.start()

    barrier = pltpu.get_barrier_semaphore()
    peers = [{"grp": at_z(d), "arch": pair + h} for d in (1, -1) for h in (0, 1)]
    peers += [{"grp": at_z(d), "arch": pair + h} for d in (2, -2) for h in (0, 1)]
    peers += [{"tile": at_tile(j), "arch": pair + h} for j in range(1, nt) for h in (0, 1)]
    peers += [{"arch": lax.rem(a + j, na)} for j in range(1, na)]
    for peer in peers:
        pl.semaphore_signal(barrier, inc=1, device_id=peer, device_id_type=MESH)
    loads[0].wait()
    pl.semaphore_wait(barrier, len(peers))

    def uz():
        rows = pl.ds(pl.multiple_of((2 * t + core) * up, 128), up)
        return remote(u.at[odd, rows], u.at[odd, rows], uz_send, uz_recv, grp=z_pair)

    def foreign(tile, h):
        return u.at[1 - odd, pl.ds(pl.multiple_of((2 * tile + h) * up, 128), up)]

    def ut(j):
        return remote(foreign(t, core), foreign(t, core), ut_send.at[j], ut_recv.at[j], tile=at_tile(j))

    def uc(j):
        rows = foreign(at_tile(nt - j), core)
        return remote(rows, rows, uc_send.at[j], uc_recv.at[j], arch=other_core)

    hop = 2 - lax.rem(z + core, 2)
    for c in range(nc):
        for h in range(2):
            src = piece.at[pl.ds(h * part + c * half, half)]
            for side, (to, slot) in enumerate(((lax.rem(z + hop, nz), nz - hop), (lax.rem(z + nz - hop, nz), hop))):
                go(remote(
                    src, pieces.at[slot, chunks[c]], f_send.at[side, h, c], g_recv.at[slot, c], grp=to, arch=pair + h
                ))

    def from_core():
        rows = pl.ds(pl.multiple_of((1 - core) * part, 16), part)
        return remote(piece.at[rows], pieces.at[0], x_send, x_recv, arch=other_core)

    @pl.when(same)
    def _():
        from_core().start()
        pieces[0] = piece[pl.ds(pl.multiple_of(core * part, 16), part), :]

    loads[2].wait()
    go(uz())
    for load in (loads[1], *loads[3:]):
        load.wait()

    def urows(d):
        return pl.ds(pl.multiple_of(at_z(d) * db, 128), db)

    own_rows = pl.ds(pl.multiple_of(t * ra, ra), ra)

    def act_product():
        total = dot(act[...], u[odd, urows(0), :])
        for d in range(1, nz):
            remote(act, acts.at[d], ar_send.at[d], ar_recv.at[d], grp=at_z(d)).wait_recv()
            total += dot(acts[d], u[odd, urows(-d), :])
        aprime[own_rows, :] = total.astype(BF16)
        for j in far_first:
            go(remote(aprime.at[own_rows], aprime.at[own_rows], a_send.at[j], a_recv.at[j], tile=at_tile(j)))

    def arrive(slot, c):
        remote(piece.at[chunks[c]], pieces.at[slot, chunks[c]], g_send.at[slot, c], g_recv.at[slot, c], grp=z).wait_recv()

    def forward(slot, c, d):
        to = (slot - d) % nz
        go(remote(
            pieces.at[slot, chunks[c]], pieces.at[to, chunks[c]], g_send.at[to, c], g_recv.at[to, c], grp=at_z(d)
        ))

    v[...] = vt[...].T

    @pl.when(jnp.logical_not(same))
    def _():
        from_core().wait_recv()

    acc[odd] = dot(pieces[0], u[odd, urows(0), :])
    ready = [0]
    for step in range(reach):
        new = []
        if step == reach - 1:
            for j in range(nt):
                if j:
                    ut_from = foreign(at_tile(nt - j), core)
                    remote(ut_from, ut_from, ut_send.at[j], ut_recv.at[j], tile=at_tile(j)).wait_recv()
                go(uc(j))

            @pl.when(same)
            def _():
                remote(eig, eig_pair, e_send, e_recv, grp=z_pair).start()

        for c in range(nc):
            for far in (0, 1):
                for side, d in enumerate((2, -2)):
                    last = reach if far else reach - (c % 2 != side)
                    if step >= last:
                        continue
                    dist = 2 * step + (1 if far else 2)
                    slot = (-dist if side == 0 else dist) % nz
                    arrive(slot, c)
                    if step + 1 < last:
                        forward(slot, c, d)
                    if slot not in new:
                        new.append(slot)
        if step == reach - 1:
            for j in range(nt):
                rows = foreign(at_tile(nt - j), 1 - core)
                remote(rows, rows, uc_send.at[j], uc_recv.at[j], arch=other_core).wait_recv()
        else:
            if step == 0:
                uz_rows = foreign(t, core)
                remote(uz_rows, uz_rows, uz_send, uz_recv, grp=z_pair).wait_recv()
                for j in far_first:
                    go(ut(j))
        for slot in new:
            acc[odd] += dot(pieces[slot], u[odd, urows(slot), :])
        ready += new
    total = dot(pieces[0], u[1 - odd, urows(0), :])
    for slot in ready[1:]:
        total += dot(pieces[slot], u[1 - odd, urows(slot), :])
    ybuf[1 - odd] = total.astype(BF16)
    ybuf[odd] = acc[odd].astype(BF16)

    def rin_rows(tile, h):
        return pl.ds(pl.multiple_of(tile * fb + h * part, 16), part)

    def tile_gather(j, e):
        rows = rin.at[rin_rows(t, core)]
        return remote(
            ybuf.at[e], rows, t_send.at[j, e], t_recv.at[j, core], tile=at_tile(j), arch=pair + e
        )

    for j in far_first:
        for e in range(2):
            go(tile_gather(j, e))
    cross = remote(
        ybuf.at[1 - core], rin.at[rin_rows(t, core)], t_send.at[0, 0], t_recv.at[0, core], arch=other_core
    )
    go(cross)
    rin[rin_rows(t, core), :] = ybuf[core]
    for d in sorted(range(1, nz), key=lambda k: -min(k, nz - k)):
        go(remote(act, acts.at[d], ar_send.at[d], ar_recv.at[d], grp=at_z(d)))

    @pl.when(jnp.logical_not(same))
    def _():
        remote(eig, eig_pair, e_send, e_recv, grp=z_pair).wait_recv()
        inv[...] = 1.0 / (eig_pair[...] + damping)

    @pl.when(same)
    def _():
        inv[...] = 1.0 / (eig[...] + damping)

    def tile_wait(j, h):
        rows = rin.at[rin_rows(at_tile(nt - j), h)]
        remote(rows, rows, t_send.at[j, 0], t_recv.at[j, h], arch=other_core).wait_recv()

    tile_wait(0, 1 - core)
    for j in range(1, nt):
        for h in range(2):
            tile_wait(j, h)
    scaled = (dot(vt[...], rin[...]) * inv[...]).astype(BF16)

    def tile_scatter(j, h):
        src = outgoing.at[rin_rows(at_tile(j), h)]
        return remote(src, arrived.at[j, core], s_send.at[j, h], s_recv.at[j, core], tile=at_tile(j), arch=pair + h)

    def block(j):
        rows = pl.ds(pl.multiple_of(at_tile(j) * fb, 16), fb)
        outgoing[rows, :] = dot(v[rows, :], scaled).astype(BF16)

    for j in far_first:
        block(j)
        for h in range(2):
            go(tile_scatter(j, h))
    block(0)
    go(remote(
        outgoing.at[rin_rows(t, 1 - core)], arrived.at[0, core], s_send.at[0, 0], s_recv.at[0, core], arch=other_core
    ))
    arrived[0, core] = outgoing[rin_rows(t, core), :]

    def scatter_wait(j, e):
        dst = arrived.at[j, e]
        remote(dst, dst, s_send.at[j, 0], s_recv.at[j, e], arch=other_core).wait_recv()

    scatter_wait(0, 1 - core)
    for j in range(1, nt):
        for e in range(2):
            scatter_wait(j, e)
    for e in range(2):
        total = arrived[0, e].astype(F32)
        for j in range(1, nt):
            total += arrived[j, e].astype(F32)
        restored[e] = total.astype(BF16)

    def share(d):
        rows = urows(d)
        return dot_last(restored[0], u[0, rows, :]) + dot_last(restored[1], u[1, rows, :])

    def lasts(far, side):
        return tuple(reach if far else reach - (c % 2 != side) for c in range(nc))

    def scatter(step, c, far, side):
        last = lasts(far, side)[c]
        src = first.at[far, side, chunks[c]] if step == 0 else chain.at[far, side, step - 1, chunks[c]]
        d = 2 if side == 0 else -2
        if step < last - 1:
            return remote(
                src, chain.at[far, side, step, chunks[c]], r_send.at[far, side, step, c],
                r_recv.at[far, side, step, c], grp=at_z(d),
            )
        return remote(
            src, final.at[side, core, chunks[c]], r0_send.at[far, side, c], rf_recv.at[side, core, c],
            grp=at_z(d // 2 if far else d), arch=mine,
        )

    def distance(step, c, far, side):
        m = 2 * (lasts(far, side)[c] - step) - far
        return m if side == 0 else -m

    core_rows = pl.ds(pl.multiple_of(core * part, 16), part)
    rall[mine, core_rows, :] = restored[odd]
    go(remote(restored.at[1 - odd], rall.at[mine, core_rows], p_send, p_recv, grp=z_pair))
    for j in range(1, na):
        go(remote(
            rall.at[mine, core_rows], rall.at[mine, core_rows], q_send.at[j, 0], q_recv.at[j, 0], arch=lax.rem(a + j, na)
        ))

    for far in (0, 1):
        for side in range(2):
            terms = {}
            for c in range(nc):
                m = distance(0, c, far, side)
                if m not in terms:
                    terms[m] = share(m)
                first[far, side, chunks[c], :] = terms[m][c * half:(c + 1) * half].astype(BF16)
                go(scatter(0, c, far, side))

    act_product()

    def spread():
        slot = rall.at[pair + 1 - odd, core_rows]
        remote(slot, slot, p_send, p_recv, grp=z_pair).wait_recv()
        for j in range(1, na):
            go(remote(slot, slot, q_send.at[j, 1], q_recv.at[j, 1], arch=lax.rem(a + j, na)))

    def token(q):
        product = dot_last(rall[q], aprime[...]) * gt[...].astype(F32)
        tokens[pl.ds(q, 1), :] = jnp.sum(product, axis=0, keepdims=True)

    def arch_wait(which):
        for j in range(1, na):
            src = lax.rem(a + (na - j), na)
            src_core = lax.rem(src, 2)
            q = src - src_core + (odd if which == 0 else 1 - odd)
            slot = rall.at[q, pl.ds(pl.multiple_of(src_core * part, 16), part)]
            remote(slot, slot, q_send.at[j, which], q_recv.at[j, which], arch=src).wait_recv()

    def scores():
        position = lax.broadcasted_iota(jnp.int32, (8, nt * ra), 1)
        lane = lax.broadcasted_iota(jnp.int32, (8, 128), 1)
        line = jnp.zeros((8, 128), F32)
        start = jnp.int32(0)
        for s in range(len_ref.shape[1]):
            end = start + len_ref[0, s]
            inside = jnp.logical_and(position >= start, position < end)
            one = jnp.sum(jnp.where(inside, tokens[...], 0.0), axis=1, keepdims=True)
            line = jnp.where(lane == s, one, line)
            start = end
        seq_tile[t] = line
        for j in far_first:
            go(remote(seq_tile.at[t], seq_tile.at[t], pt_send.at[j], pt_recv.at[j], tile=at_tile(j)))

    def sum_tile():
        for j in range(1, nt):
            slot = seq_tile.at[at_tile(nt - j)]
            remote(slot, slot, pt_send.at[j], pt_recv.at[j], tile=at_tile(j)).wait_recv()
        total = seq_tile[0]
        for i in range(1, nt):
            total += seq_tile[i]
        seq_z[z] = total
        for d in sorted(range(1, nz), key=lambda k: -min(k, nz - k)):
            go(remote(seq_z.at[z], seq_z.at[z], pz_send.at[d], pz_recv.at[d], grp=at_z(d)))

    def sum_z():
        for d in range(1, nz):
            slot = seq_z.at[at_z(-d)]
            remote(slot, slot, pz_send.at[d], pz_recv.at[d], grp=at_z(d)).wait_recv()
        total = seq_z[0]
        for i in range(1, nz):
            total += seq_z[i]
        lane = lax.broadcasted_iota(jnp.int32, (1, 128), 1)
        sizes = jnp.ones((1, 128), F32)
        for s in range(len_ref.shape[1]):
            sizes = jnp.where(lane == s, len_ref[0, s].astype(F32), sizes)
        score_ref[...] = (total / sizes)[:na, : len_ref.shape[1]]

    spread()
    for step in range(1, reach):
        for far in (0, 1):
            for side in range(2):
                terms = {}
                for c in range(nc):
                    if step < lasts(far, side)[c]:
                        m = distance(step, c, far, side)
                        if m not in terms:
                            terms[m] = share(m)
                for c in range(nc):
                    if step >= lasts(far, side)[c]:
                        continue
                    m = distance(step, c, far, side)
                    scatter(step - 1, c, far, side).wait_recv()
                    got = chain[far, side, step - 1, chunks[c], :].astype(F32)
                    chain[far, side, step - 1, chunks[c], :] = (
                        got + terms[m][c * half:(c + 1) * half]
                    ).astype(BF16)
                    go(scatter(step, c, far, side))
        if step == 1:
            own[...] = share(0)

            @pl.when(jnp.logical_not(same))
            def _():
                own_pair[0] = own[...].astype(BF16)
                remote(own_pair.at[0], own_pair.at[1], o_send, o_recv, arch=other_core).start()

            tokens[...] = jnp.zeros_like(tokens)
            for j in range(1, nt):
                place = aprime.at[pl.ds(pl.multiple_of(at_tile(nt - j) * ra, ra), ra)]
                remote(place, place, a_send.at[j], a_recv.at[j], tile=at_tile(j)).wait_recv()
            for which in range(2):
                arch_wait(which)
                q = odd if which == 0 else 1 - odd
                token(q)
                token(2 + q)
            scores()
        if step == max(reach - 2, 2):
            sum_tile()

    if reach == 2:
        sum_tile()
    for copy in sent:
        copy.wait_send()

    for side in range(2):
        for h in range(2):
            for c in range(nc):
                slot = final.at[side, h, chunks[c]]
                remote(slot, slot, r0_send.at[0, side, c], rf_recv.at[side, h, c], grp=z_pair).wait_recv()
    for h in range(2):
        total = final[0, h].astype(F32) + final[1, h].astype(F32)
        pre_ref[pl.ds(h * part, part), :] = total.astype(BF16)

    @pl.when(same)
    def _():
        remote(own_pair.at[0], own_pair.at[1], o_send, o_recv, arch=other_core).wait_recv()
        for h, term in ((core, own[...]), (1 - core, own_pair[1].astype(F32))):
            total = final[0, h].astype(F32) + final[1, h].astype(F32) + term
            pre_ref[pl.ds(pl.multiple_of(h * part, 16), part), :] = total.astype(BF16)

    sum_z()

    @pl.when(same)
    def _():
        from_core().wait_send()
        remote(eig, eig_pair, e_send, e_recv, grp=z_pair).wait_send()

    @pl.when(jnp.logical_not(same))
    def _():
        remote(own_pair.at[0], own_pair.at[1], o_send, o_recv, arch=other_core).wait_send()


def per_device(nz, nt, na, query_grads, input_basis, output_basis, eigenvalues, activations, gradients, seq_lengths):
    fb, db = query_grads.shape[1:]
    d_all, f_all = input_basis.shape[0], output_basis.shape[0]
    archive = activations.shape[0]
    ra = archive // nt
    part = fb // 2
    nc = 2
    reach = nz // 4
    anywhere = pl.BlockSpec(memory_space=pl.ANY)
    dma = pltpu.SemaphoreType.DMA
    vmem = pltpu.VMEM
    one = dma(())
    pre, scores = pl.pallas_call(
        functools.partial(kernel, nz, nt, na),
        out_shape=(jax.ShapeDtypeStruct((fb, db), BF16), jax.ShapeDtypeStruct((na, seq_lengths.shape[1]), F32)),
        in_specs=[anywhere] * 6 + [pl.BlockSpec(memory_space=pltpu.SMEM)],
        out_specs=[pl.BlockSpec(memory_space=pltpu.VMEM)] * 2,
        scratch_shapes=[
            vmem((fb, db), BF16),
            vmem((nz, part, db), BF16),
            vmem((ra, db), BF16),
            vmem((nz, ra, db), BF16),
            vmem((2, d_all, db), BF16),
            vmem((fb, f_all), BF16),
            vmem((f_all, fb), BF16),
            vmem((fb, db), F32),
            vmem((fb, db), F32),
            vmem((fb, db), F32),
            vmem((fb, archive), BF16),
            vmem((2, part, db), F32),
            vmem((2, part, db), BF16),
            vmem((f_all, db), BF16),
            vmem((archive, db), BF16),
            vmem((f_all, db), BF16),
            vmem((nt, 2, part, db), BF16),
            vmem((2, part, db), BF16),
            vmem((na, fb, db), BF16),
            vmem((2, 2, part, db), BF16),
            vmem((2, 2, reach, part, db), BF16),
            vmem((2, 2, part, db), BF16),
            vmem((part, db), F32),
            vmem((2, part, db), BF16),
            vmem((8, archive), F32),
            vmem((nt, 8, 128), F32),
            vmem((nz, 8, 128), F32),
            dma((6,)), dma((2, 2, nc)), dma((nz, nc)), dma((nz, nc)), one, one,
            dma((nz,)), dma((nz,)),
            one, one, dma((nt,)), dma((nt,)), dma((nt,)), dma((nt,)),
            one, one, dma((nt, 2)), dma((nt, 2)), dma((nt,)), dma((nt,)), dma((nt, 2)), dma((nt, 2)),
            one, one, dma((na, 2)), dma((na, 2)),
            dma((2, 2, nc)), dma((2, 2, reach, nc)), dma((2, 2, reach, nc)), dma((2, 2, nc)), one, one,
            dma((nt,)), dma((nt,)), dma((nz,)), dma((nz,)),
        ],
        compiler_params=pltpu.CompilerParams(
            collective_id=0, has_side_effects=True, vmem_limit_bytes=54 * 2**20
        ),
    )(query_grads, input_basis, output_basis.T, eigenvalues, activations, gradients.T, seq_lengths)
    return pre.T[None], scores


def solution(mesh):
    nz, nt, na = mesh.shape["grp"], mesh.shape["tile"], mesh.shape["arch"]
    return jax.shard_map(
        functools.partial(per_device, nz, nt, na),
        mesh=mesh,
        in_specs=(
            P("arch", "tile", "grp"),
            P(None, "grp"),
            P(None, "tile"),
            P("tile", "grp"),
            P("arch", "grp"),
            P("arch", "tile"),
            P("arch", None),
        ),
        out_specs=(P("arch", "grp", "tile"), P(None, "arch")),
        check_vma=False,
    )
```
